256 devices in a mesh: prow: 64 (over x, z, core), pcol: 4 (over y).
Axes of the slice: x: 4, y: 4, z: 8, core: 2. Of those that a mesh axis runs over, the one named last changes fastest.
Arguments:
- matrix: float32 [24576, 15360], P('prow', 'pcol'), may hold values from -6 to 6
- lower_panel: float32 [24576, 256], P(('prow', 'pcol')), may hold values from -0.375 to 0.375
- inverse: float32 [256, 256], P('pcol'), as said below
- pivots: int32 [256], replicated, may hold values from 0 to 24575, as said below
Outputs:
- updated: float32 [24576, 15360], P('prow', 'pcol')
The draws below stay inside these ranges and needn't reach their ends.
Inputs may be any that keep to these rules, and one draw needn't show every extreme that they name: pivots[i] is at least i; some entry equals 24575. inverse is unit lower triangular.
All inputs are finite; a program needn't handle non-finite values.
Results may differ from the reference program's by a relative error of at most 0.0003.
Values sent between devices are 32-bit elements; how exact they have to be, the bound alone decides.
A program may use at most 64 MiB of HBM per device.

```python
import jax
import jax.numpy as jnp
from jax import lax

BLOCK = 128
NB = 256
ROWS_DEV = 384
ROWS = 24576
COLS = 15360
N_PROW = 64


def draw_inverse(key, part):
    values = jax.random.normal(key, (NB, NB), jnp.float32)
    lower_part = jnp.tril(values, -1) * NB ** (-0.5)
    return (jnp.eye(NB, dtype=jnp.float32) + lower_part).astype(jnp.float32)


def draw_pivots(key, part):
    first_key = jax.random.fold_in(key, 11)
    second_key = jax.random.fold_in(key, 23)
    columns = jnp.arange(NB, dtype=jnp.int32)
    raw_bits = jax.random.randint(first_key, (NB,), 0, 1073741824, dtype=jnp.int32)
    spans = ROWS - columns
    picked = columns + raw_bits % spans
    forced = jax.random.randint(second_key, (), 0, NB, dtype=jnp.int32)
    return jnp.where(columns == forced, ROWS - 1, picked).astype(jnp.int32)


def steps_of(key, dims, split, least, top_value):
    level, own = 1.0, jax.random.fold_in(key, 6)
    for position, shards_of in split:
        heights = jnp.exp(jax.random.uniform(jax.random.fold_in(own, position), (shards_of,), jnp.float32, least / len(split), top_value / len(split)))
        level = level * jnp.repeat(heights, dims[position] // shards_of).reshape([-1 if axis == position else 1 for axis in range(len(dims))])
    return level


def bell_draw(own_key, dims, deviation, bound, pieces=(), kind=jnp.bfloat16):
    entries = jax.random.normal(own_key, dims, jnp.float32) * deviation
    if len(pieces) > 0:
        entries = steps_of(own_key, dims, pieces, -0.22, 0.18) * entries
    return jnp.clip(entries, min=-bound, max=bound).astype(kind)


def setup_inputs(seed: int = 0) -> dict:
    key_list = jax.random.split(jax.random.key(seed), 5)
    return {
        "matrix": bell_draw(key_list[0], (ROWS, COLS), 1.0, 6.0, ((0, 64), (1, 4)), jnp.float32),
        "lower_panel": bell_draw(key_list[1], (ROWS, NB), NB ** -0.5, 0.375, ((0, 256),), jnp.float32),
        "inverse": draw_inverse(jax.random.fold_in(key_list[4], 71), 0),
        "pivots": draw_pivots(jax.random.fold_in(key_list[4], 71), 0),
    }


def storage(global_rows):
    blocks = global_rows // BLOCK
    return ((blocks % N_PROW) * ROWS_DEV + (blocks // N_PROW) * BLOCK + global_rows % BLOCK).astype(jnp.int32)


def swaps(pivots, total_rows):
    def turn(turn_index, row_order):
        target = pivots[turn_index]
        first_val = row_order[turn_index]
        second_val = row_order[target]
        row_order = row_order.at[turn_index].set(second_val)
        return row_order.at[target].set(first_val)
    return lax.fori_loop(0, NB, turn, jnp.arange(total_rows, dtype=jnp.int32))


def reference(matrix, lower_panel, inverse, pivots):
    total_rows = ROWS_DEV * N_PROW
    row_order = swaps(pivots, total_rows)
    top_rows = matrix[storage(row_order[:NB])]
    u_rows = jnp.dot(inverse, top_rows, precision=lax.Precision.HIGHEST, preferred_element_type=jnp.float32)

    def one_shard(shard_row):
        local_rows = jnp.arange(ROWS_DEV, dtype=jnp.int32)
        global_rows = ((local_rows // BLOCK) * N_PROW + shard_row) * BLOCK + local_rows % BLOCK
        source_rows = matrix[storage(row_order[global_rows])]
        panel_rows = lax.dynamic_slice_in_dim(lower_panel, (shard_row * ROWS_DEV).astype(jnp.int32), ROWS_DEV, 0)
        result = source_rows - jnp.dot(panel_rows, u_rows, precision=lax.Precision.HIGHEST, preferred_element_type=jnp.float32)
        top_vals = u_rows[jnp.clip(global_rows, 0, NB - 1)]
        return jnp.where((global_rows < NB)[:, None], top_vals, result)

    shards = lax.map(one_shard, jnp.arange(N_PROW, dtype=jnp.int32))
    return shards.reshape(total_rows, shards.shape[2])
```

```python
import functools

import jax
import jax.numpy as jnp
from jax import lax
from jax.experimental import pallas as pl
from jax.experimental.pallas import tpu as pltpu
from jax.sharding import PartitionSpec as P

BLOCK = 128
NB = 256
CAP = 16
NX, NZ, NY = 4, 8, 4
CHIPS = NX * NZ
TILES = 30
COLS = TILES * 128
ROWS = 384
MESH = pl.DeviceIdType.MESH
f32 = jnp.float32
i32 = jnp.int32
bf16 = jnp.bfloat16


def plan_kernel(p_ref, mat, tab, comp, tab_s, sem, row_sems):
    me = lax.axis_index("prow")
    core = (me % 2).astype(f32)
    mef = me.astype(f32)
    big = (NB, NB)
    I = lax.broadcasted_iota(i32, big, 0)
    J = lax.broadcasted_iota(i32, big, 1)
    Jf = J.astype(f32)
    eye = I == J
    lt = J < I
    PB = jnp.broadcast_to(p_ref[...].astype(f32), big)

    def to_col(row_b):
        return jnp.sum(jnp.where(eye, row_b, 0.0), axis=1, keepdims=True)

    def to_row(col):
        return jnp.sum(jnp.where(eye, jnp.broadcast_to(col, big), 0.0), axis=0, keepdims=True)

    def pick(col_idx, row_vals):
        return jnp.sum(jnp.where(Jf == col_idx, jnp.broadcast_to(row_vals, big), 0.0), axis=1, keepdims=True)

    p_col = to_col(PB)
    eq = (p_col == PB) & lt
    prev = jnp.max(jnp.where(eq, Jf, -1.0), axis=1, keepdims=True)
    later = jnp.max(jnp.where(eq, 1.0, 0.0), axis=0, keepdims=True)
    par = jnp.max(jnp.where((PB == I.astype(f32)) & lt, Jf, -1.0), axis=1, keepdims=True)
    icol = lax.broadcasted_iota(i32, (NB, 1), 0).astype(f32)
    root = jnp.where(par < 0.0, icol, par)

    def more(state):
        return state[1] > 0.0

    def double(state):
        r, _ = state
        nr = pick(r, to_row(r))
        return nr, jnp.max(r - nr)

    root, _ = lax.while_loop(more, double, (root, jnp.float32(1.0)))
    c_row = to_row(root)
    ts = jnp.where(prev >= 0.0, pick(prev, c_row), p_col)
    tsi = ts.astype(i32)
    owner_i = lax.shift_right_logical(tsi, 7) & 63
    owner = owner_i.astype(f32)
    lidx = (lax.shift_right_logical(tsi, 13) * BLOCK + (tsi & 127)).astype(f32)
    slot = jnp.sum(jnp.where((owner == jnp.broadcast_to(to_row(owner), big)) & lt, 1.0, 0.0), axis=1, keepdims=True)
    last_c = jnp.broadcast_to(jnp.where(later > 0.0, 0.0, c_row), big)
    w = jnp.sum(jnp.where(ts == PB, last_c, 0.0), axis=1, keepdims=True)
    out_row = ts >= float(NB)
    flag = jnp.max(slot) >= float(CAP)
    mine_core = (owner_i & 1).astype(f32) == core
    chip = lax.shift_right_logical(owner_i, 1).astype(f32)
    flat = jnp.where(mine_core, chip * CAP + slot, float(CHIPS * CAP))
    flat = jnp.minimum(flat, float(CHIPS * CAP))
    src_row = to_row(flat)
    S = lax.broadcasted_iota(i32, (NB, CHIPS * CAP), 1).astype(f32)
    ret = jnp.sum(jnp.where((flat == S) & (slot < float(CAP)) & out_row, w, 0.0), axis=0, keepdims=True)
    ret = jnp.clip(ret, 0.0, NB - 1.0)
    K = lax.broadcasted_iota(i32, (NB, 128), 1).astype(f32)
    own = (owner == mef) & (slot == K)
    gath = jnp.max(jnp.where(own, lidx, 0.0), axis=0, keepdims=True)
    dest = jnp.max(jnp.where(own & out_row, lidx, -1.0), axis=0, keepdims=True)
    tab[...] = jnp.zeros((8, 512), i32)
    tab[0:1, 0:NB] = src_row.astype(i32)
    tab[1:2, :] = ret.astype(i32)
    tab[2:3, 0:128] = gath.astype(i32)
    tab[3:4, 0:128] = dest.astype(i32)
    tab[4:5, 0:NB] = to_row(ts).astype(i32)
    tab[5:6, 0:NB] = to_row(w).astype(i32)
    tab[6:7, 0:128] = jnp.broadcast_to(jnp.where(flag, 1, 0), (1, 128)).astype(i32)
    copy = pltpu.make_async_copy(tab.at[2:3, 0:128], tab_s, sem)
    copy.start()
    copy.wait()
    copies = []
    for k in range(CAP):
        row = tab_s[0, k]
        copies.append(pltpu.make_async_copy(mat.at[pl.ds(row, 1), :], comp.at[pl.ds(k, 1), :], row_sems.at[k]))
    for copy in copies:
        copy.start()
    for copy in copies:
        copy.wait()


def plan(pivots, matrix):
    vm = pl.BlockSpec(memory_space=pltpu.VMEM)
    return pl.pallas_call(
        plan_kernel,
        out_shape=(jax.ShapeDtypeStruct((8, 512), i32), jax.ShapeDtypeStruct((CAP, COLS), f32)),
        in_specs=[vm, pl.BlockSpec(memory_space=pl.ANY)],
        out_specs=(vm, vm),
        scratch_shapes=[
            pltpu.SMEM((1, 128), i32),
            pltpu.SemaphoreType.DMA,
            pltpu.SemaphoreType.DMA((CAP,)),
        ],
        compiler_params=pltpu.CompilerParams(vmem_limit_bytes=24 << 20),
        name="plan",
    )(pivots.reshape(1, NB), matrix)


def move_kernel(tab, comp, mat, lp, inv, u, sw, lg, nr, top, psib, invf, orig, ret,
                s_nr, r_nr, s_or, r_or, s_y, r_inv, r_lp, s_sib, r_psib, r_osib, s_ret, r_ret, s_ring, r_tile, r_usib):
    me = lax.axis_index("prow")
    yy = lax.axis_index("pcol")
    core = me % 2
    chip = me // 2
    x = chip // NZ
    z = chip % NZ

    def tile_of(xx, zz):
        return (zz + NZ - 1) % NZ * NX + (xx + NX - 1) % NX

    def at(xx, zz, cc):
        return {"prow": (xx * NZ + zz) * 2 + cc, "pcol": yy}

    def peer(dchip):
        return {"prow": dchip * 2 + core, "pcol": yy}

    sibling = at(x, z, 1 - core)
    jt = tile_of(x, z)
    holder = jt < TILES

    def remote(src, dst, ss, rs, dev):
        return pltpu.make_async_remote_copy(src_ref=src, dst_ref=dst, send_sem=ss, recv_sem=rs, device_id=dev, device_id_type=MESH)

    def drain(ref, sem):
        pltpu.make_async_copy(ref, ref, sem).wait()

    barrier = pltpu.get_barrier_semaphore()

    def greet(k, _):
        pl.semaphore_signal(barrier, inc=1, device_id=peer((chip + k) % CHIPS), device_id_type=MESH)
        return 0

    lax.fori_loop(1, CHIPS, greet, 0)
    pl.semaphore_signal(barrier, inc=1, device_id=sibling, device_id_type=MESH)
    for k in range(1, NY):
        pl.semaphore_signal(barrier, inc=1, device_id={"prow": me, "pcol": (yy + k) % NY}, device_id_type=MESH)
    pl.semaphore_wait(barrier, CHIPS - 1 + 1 + NY - 1)

    def send_new(k, _):
        d = (chip + k) % CHIPS
        j = tile_of(d // NZ, d % NZ)

        @pl.when(j < TILES)
        def _():
            remote(
                comp.at[:, pl.ds(pl.multiple_of(j * 128, 128), 128)],
                nr.at[pl.ds(pl.multiple_of(chip * CAP, CAP), CAP), :],
                s_nr, r_nr, peer(d),
            ).start()

        return 0

    lax.fori_loop(1, CHIPS, send_new, 0)

    @pl.when(holder)
    def _():
        pltpu.make_async_copy(
            comp.at[:, pl.ds(pl.multiple_of(jt * 128, 128), 128)],
            nr.at[pl.ds(pl.multiple_of(chip * CAP, CAP), CAP), :],
            r_nr,
        ).start()

    for k in range(1, NY):
        dev = {"prow": me, "pcol": (yy + k) % NY}
        remote(inv, invf.at[yy], s_y.at[0], r_inv, dev).start()
        remote(lp, lg.at[yy], s_y.at[1], r_lp, dev).start()
    pltpu.make_async_copy(inv, invf.at[yy], r_inv).start()
    pltpu.make_async_copy(lp, lg.at[yy], r_lp).start()

    @pl.when(chip == 0)
    def _():
        def send_orig(k, _):
            j = tile_of(k // NZ, k % NZ)

            @pl.when(j < TILES)
            def _():
                remote(
                    mat.at[pl.ds(0, BLOCK), pl.ds(pl.multiple_of(j * 128, 128), 128)],
                    orig.at[pl.ds(pl.multiple_of(core * BLOCK, BLOCK), BLOCK), :],
                    s_or, r_or, peer(k),
                ).start()

            return 0

        lax.fori_loop(1, CHIPS, send_orig, 0)

    nr[pl.ds(CHIPS * CAP, 8), :] = jnp.zeros((8, 128), f32)

    my_half = pl.ds(pl.multiple_of(core * BLOCK, BLOCK), BLOCK)
    other_half = pl.ds(pl.multiple_of((1 - core) * BLOCK, BLOCK), BLOCK)

    drain(invf, r_inv)

    @pl.when(holder)
    def _():
        drain(nr.at[pl.ds(0, CHIPS * CAP), :], r_nr)

        def arrange(b, _):
            for t in range(8):
                i = b * 8 + t
                top[pl.ds(i, 1), :] = nr[pl.ds(tab[0, i], 1), :]
            return 0

        lax.fori_loop(0, NB // 8, arrange, 0)
        full = invf[...].reshape(NB, NB)
        top[...] = jnp.dot(full, top[...], precision=lax.Precision.HIGHEST, preferred_element_type=f32)
        back = remote(top.at[other_half, :], psib, s_sib.at[0], r_psib, sibling)
        back.start()
        back.wait()
        u[jt, my_half, :] = top[my_half, :] + psib[...]

    @pl.when(jnp.logical_not(holder))
    def _():
        u[jt, my_half, :] = jnp.zeros((BLOCK, 128), f32)

    def rows_of(part):
        if part is None:
            return my_half
        return pl.ds(pl.multiple_of(core * BLOCK + part * 64, 64), 64)

    def push(xx, zz, part, tx, tz):
        j = tile_of(xx, zz)
        ref = u.at[j, rows_of(part), :]
        remote(ref, ref, s_ring, r_tile.at[j], at(tx, tz, core)).start()

    def share(xx, zz):
        j = tile_of(xx, zz)
        ref = u.at[j, my_half, :]
        remote(ref, ref, s_sib.at[1], r_usib, sibling).start()

    def arrived(xx, zz):
        j = tile_of(xx, zz)
        drain(u.at[j, my_half, :], r_tile.at[j])

    xp, xm = (x + 1) % NX, (x + NX - 1) % NX
    zp, zm = (z + 1) % NZ, (z + NZ - 1) % NZ

    def give_back():
        @pl.when(holder)
        def _():
            drain(orig.at[my_half, :], r_or)
            ref = orig.at[my_half, :]
            copy = remote(ref, ref, s_sib.at[2], r_osib, sibling)
            copy.start()
            copy.wait()

            def arrange(b, _):
                for t in range(8):
                    i = b * 8 + t
                    ret[pl.ds(i, 1), :] = orig[pl.ds(tab[1, i], 1), :]
                return 0

            lax.fori_loop(0, CHIPS * CAP // 8, arrange, 0)

            def send(k, _):
                d = (chip + k) % CHIPS
                remote(ret.at[pl.ds(pl.multiple_of(d * CAP, CAP), CAP), :], sw.at[jt], s_ret, r_ret, peer(d)).start()
                return 0

            lax.fori_loop(1, CHIPS, send, 0)
            pltpu.make_async_copy(ret.at[pl.ds(pl.multiple_of(chip * CAP, CAP), CAP), :], sw.at[jt], r_ret).start()

    def x_neighbours(zz):
        arrived(xm, zz)
        push(xm, zz, 0, xp, z)
        share(xm, zz)
        arrived(xp, zz)
        push(xp, zz, 1, xm, z)
        share(xp, zz)

    def x_far(zz):
        arrived((x + 2) % NX, zz)
        share((x + 2) % NX, zz)

    def z_step(xx, s, onward):
        for sign in (1, -1):
            zz = (z - sign * s + NZ) % NZ
            if s == NZ // 2 and sign == -1:
                continue
            arrived(xx, zz)
            if s < NZ // 2 - 1:
                push(xx, zz, None, x, (z + sign + NZ) % NZ)
            elif s == NZ // 2 - 1:
                push(xx, zz, 0 if sign == 1 else 1, x, (z + sign + NZ) % NZ)
            if onward:
                push(xx, zz, None, xp, z)
                push(xx, zz, None, xm, z)
            share(xx, zz)

    push(x, z, None, x, zp)
    push(x, z, None, x, zm)
    push(x, z, None, xp, z)
    push(x, z, None, xm, z)
    share(x, z)

    @pl.when(core == 0)
    def _():
        def zs(s):
            return [z] if s == 0 else [(z + NZ - s) % NZ] if s == NZ // 2 else [(z + NZ - s) % NZ, (z + s) % NZ]

        for s in range(1, NZ // 2 + 3):
            if s <= NZ // 2:
                z_step(x, s, True)
            if s - 1 <= NZ // 2:
                for zz in zs(s - 1):
                    x_neighbours(zz)
            if s - 2 >= 0:
                for zz in zs(s - 2):
                    x_far(zz)
            if s == 3:
                give_back()

    @pl.when(core == 1)
    def _():
        arrived(xm, z)
        push(xm, z, 0, xp, z)
        push(xm, z, None, x, zp)
        push(xm, z, None, x, zm)
        share(xm, z)
        arrived(xp, z)
        push(xp, z, 1, xm, z)
        push(xp, z, None, x, zp)
        push(xp, z, None, x, zm)
        share(xp, z)
        xf = (x + 2) % NX
        arrived(xf, z)
        push(xf, z, None, x, zp)
        push(xf, z, None, x, zm)
        share(xf, z)
        for s in range(1, NZ // 2 + 1):
            for xx in (x, xm, xp, xf):
                z_step(xx, s, False)
            if s == 2:
                give_back()

    drain(lg, r_lp)
    drain(sw.at[pl.ds(0, TILES)], r_ret)
    drain(u.at[pl.ds(0, CHIPS), other_half, :], r_usib)
    drain(u.at[pl.ds(0, CHIPS), my_half, :], s_sib.at[1])
    drain(u.at[pl.ds(0, CHIPS - 1), my_half, :], s_ring)
    drain(invf.at[pl.ds(0, NY - 1)], s_y.at[0])
    drain(lg.at[pl.ds(0, NY - 1)], s_y.at[1])

    @pl.when(holder)
    def _():
        drain(nr.at[pl.ds(0, (TILES - 1) * CAP), :], s_nr)
        drain(ret.at[pl.ds(0, (CHIPS - 1) * CAP), :], s_ret)

    @pl.when(jnp.logical_not(holder))
    def _():
        drain(nr.at[pl.ds(0, TILES * CAP), :], s_nr)

    @pl.when(chip == 0)
    def _():
        drain(mat.at[pl.ds(0, BLOCK), :], s_or)


def move(tab, comp, matrix, lower_panel, inverse):
    vm = pl.BlockSpec(memory_space=pltpu.VMEM)
    dma = pltpu.SemaphoreType.DMA
    return pl.pallas_call(
        move_kernel,
        out_shape=(
            jax.ShapeDtypeStruct((CHIPS, NB, 128), f32),
            jax.ShapeDtypeStruct((CHIPS, CAP, 128), f32),
            jax.ShapeDtypeStruct((NY, ROWS // NY, NB), f32),
        ),
        in_specs=[pl.BlockSpec(memory_space=pltpu.SMEM), vm, pl.BlockSpec(memory_space=pl.ANY), vm, vm],
        out_specs=(vm, vm, vm),
        scratch_shapes=[
            pltpu.VMEM((CHIPS * CAP + 8, 128), f32),
            pltpu.VMEM((NB, 128), f32),
            pltpu.VMEM((BLOCK, 128), f32),
            pltpu.VMEM((NY, NB // NY, NB), f32),
            pltpu.VMEM((NB, 128), f32),
            pltpu.VMEM((CHIPS * CAP, 128), f32),
            dma, dma, dma, dma, dma((2,)), dma, dma, dma((3,)), dma, dma, dma, dma, dma, dma((CHIPS,)), dma,
        ],
        compiler_params=pltpu.CompilerParams(collective_id=0, has_side_effects=True, vmem_limit_bytes=32 << 20),
        name="move",
    )(tab, comp, matrix, lower_panel, inverse)


def split(v):
    hi = v.astype(bf16)
    return hi, (v - hi.astype(f32)).astype(bf16)


def update_kernel(tab, mat, u, sw, lg, out, l_hi, l_lo, lu):
    me = lax.axis_index("prow")

    @pl.when(pl.program_id(0) == 0)
    def _():
        hi, lo = split(lg[...])
        l_hi[...] = hi
        l_lo[...] = lo

    uu = jnp.concatenate([u[k] for k in range(NX)], axis=1)
    u_hi, u_lo = split(uu)
    prod = functools.partial(jnp.dot, preferred_element_type=f32)
    lu[...] = prod(l_hi[...], u_hi) + (prod(l_lo[...], u_hi) + prod(l_hi[...], u_lo))
    out[...] = mat[...] - lu[...]
    for k in range(CAP):
        row = tab[3, k]

        @pl.when(row >= 0)
        def _():
            new = jnp.concatenate([sw[t, k : k + 1, :] for t in range(NX)], axis=1)
            out[pl.ds(row, 1), :] = new - lu[pl.ds(row, 1), :]

    for half in range(2):

        @pl.when(me == half)
        def _():
            out[0:BLOCK, :] = jnp.concatenate([u[k, half * BLOCK : (half + 1) * BLOCK, :] for k in range(NX)], axis=1)


def update(tab, matrix, u, sw, lg):
    width = NX * 128
    return pl.pallas_call(
        update_kernel,
        grid=(NZ,),
        out_shape=jax.ShapeDtypeStruct((ROWS, COLS), f32),
        in_specs=[
            pl.BlockSpec(memory_space=pltpu.SMEM),
            pl.BlockSpec((ROWS, width), lambda g: (0, g)),
            pl.BlockSpec((NX, NB, 128), lambda g: (g, 0, 0)),
            pl.BlockSpec((NX, CAP, 128), lambda g: (g, 0, 0)),
            pl.BlockSpec((ROWS, NB), lambda g: (0, 0)),
        ],
        out_specs=pl.BlockSpec((ROWS, width), lambda g: (0, g)),
        scratch_shapes=[pltpu.VMEM((ROWS, NB), bf16), pltpu.VMEM((ROWS, NB), bf16), pltpu.VMEM((ROWS, width), f32)],
        compiler_params=pltpu.CompilerParams(vmem_limit_bytes=32 << 20),
        name="update",
    )(tab, matrix, u, sw, lg)


def general(matrix, lg, inverse, source, moved):
    my_row = lax.axis_index("prow")
    row_count = lax.axis_size("prow")
    high = functools.partial(jnp.dot, precision=lax.Precision.HIGHEST, preferred_element_type=f32)
    local_rows = jnp.arange(ROWS, dtype=i32)
    global_rows = (local_rows // BLOCK * row_count + my_row) * BLOCK + local_rows % BLOCK
    owner = source // BLOCK % row_count
    local_index = source // BLOCK // row_count * BLOCK + source % BLOCK
    new_part = jnp.where((owner == my_row)[:, None], jnp.take(matrix, local_index, axis=0), 0.0)
    block_ids = jnp.arange(NB // BLOCK, dtype=i32)
    orig_part = jnp.where((block_ids == my_row)[:, None, None], matrix[None, :BLOCK], 0.0).reshape(NB, COLS)
    gathered, top_orig = lax.psum((new_part, orig_part), "prow")
    hit = (source[None, :] == global_rows[:, None]) & (global_rows >= NB)[:, None]
    fetch = jnp.max(jnp.where(hit, moved[None, :], -1), axis=1)
    swapped = jnp.where((fetch >= 0)[:, None], jnp.take(top_orig, jnp.clip(fetch, 0, NB - 1), axis=0), matrix)
    u_rows = high(lax.all_gather(inverse, "pcol", axis=0, tiled=True), gathered)
    result = swapped - high(lg, u_rows)
    head = lax.dynamic_slice_in_dim(u_rows, jnp.minimum(my_row, 1) * BLOCK, BLOCK, 0)
    first = jnp.where(my_row < 2, head, result[:BLOCK])
    return jnp.concatenate([first, result[BLOCK:]], axis=0)


def local(matrix, lower_panel, inverse, pivots):
    tab, comp = plan(pivots, matrix)
    u, sw, lg = move(tab, comp, matrix, lower_panel, inverse)
    lg = lg.reshape(ROWS, NB)
    return lax.cond(
        tab[6, 0] == 0,
        lambda: update(tab, matrix, u, sw, lg),
        lambda: general(matrix, lg, inverse, tab[4, :NB], tab[5, :NB]),
    )


def solution(mesh):
    return jax.shard_map(
        local,
        mesh=mesh,
        in_specs=(P("prow", "pcol"), P(("prow", "pcol"), None), P("pcol", None), P()),
        out_specs=P("prow", "pcol"),
        check_vma=False,
    )
```

```python
import functools

import jax
import jax.numpy as jnp
from jax import lax
from jax.experimental import pallas as pl
from jax.experimental.pallas import tpu as pltpu
from jax.sharding import PartitionSpec as P

BLOCK = 128
NB = 256
CAP = 16
NX, NZ, NY = 4, 8, 4
N_PROW = 64
CHIPS = NX * NZ
AWAY = (4, 3, 5, 2, 6, 1, 7)
TILES = 30
COLS = TILES * 128
ROWS = 384
MESH = pl.DeviceIdType.MESH
f32 = jnp.float32
i32 = jnp.int32
bf16 = jnp.bfloat16


def plan_kernel(p_ref, mat, tab, comp, tab_s, sem, row_sems):
    me = lax.axis_index("prow")
    core = (me % 2).astype(f32)
    mef = me.astype(f32)
    big = (NB, NB)
    I = lax.broadcasted_iota(i32, big, 0)
    J = lax.broadcasted_iota(i32, big, 1)
    Jf = J.astype(f32)
    eye = I == J
    lt = J < I
    PB = jnp.broadcast_to(p_ref[...].astype(f32), big)

    def to_col(row_b):
        return jnp.sum(jnp.where(eye, row_b, 0.0), axis=1, keepdims=True)

    def to_row(col):
        return jnp.sum(jnp.where(eye, jnp.broadcast_to(col, big), 0.0), axis=0, keepdims=True)

    def pick(col_idx, row_vals):
        return jnp.sum(jnp.where(Jf == col_idx, jnp.broadcast_to(row_vals, big), 0.0), axis=1, keepdims=True)

    p_col = to_col(PB)
    eq = (p_col == PB) & lt
    prev = jnp.max(jnp.where(eq, Jf, -1.0), axis=1, keepdims=True)
    later = jnp.max(jnp.where(eq, 1.0, 0.0), axis=0, keepdims=True)
    par = jnp.max(jnp.where((PB == I.astype(f32)) & lt, Jf, -1.0), axis=1, keepdims=True)
    icol = lax.broadcasted_iota(i32, (NB, 1), 0).astype(f32)
    root = jnp.where(par < 0.0, icol, par)

    def more(state):
        return state[1] > 0.0

    def double(state):
        r, _ = state
        nr = pick(r, to_row(r))
        return nr, jnp.max(r - nr)

    root, _ = lax.while_loop(more, double, (root, jnp.float32(1.0)))
    c_row = to_row(root)
    ts = jnp.where(prev >= 0.0, pick(prev, c_row), p_col)
    tsi = ts.astype(i32)
    owner_i = lax.shift_right_logical(tsi, 7) & 63
    owner = owner_i.astype(f32)
    lidx = (lax.shift_right_logical(tsi, 13) * BLOCK + (tsi & 127)).astype(f32)
    slot = jnp.sum(jnp.where((owner == jnp.broadcast_to(to_row(owner), big)) & lt, 1.0, 0.0), axis=1, keepdims=True)
    last_c = jnp.broadcast_to(jnp.where(later > 0.0, 0.0, c_row), big)
    w = jnp.sum(jnp.where(ts == PB, last_c, 0.0), axis=1, keepdims=True)
    out_row = ts >= float(NB)
    flag = jnp.max(slot) >= float(CAP)
    mine_core = (owner_i & 1).astype(f32) == core
    chip = lax.shift_right_logical(owner_i, 1).astype(f32)
    flat = jnp.where(mine_core, chip * CAP + slot, float(CHIPS * CAP))
    flat = jnp.minimum(flat, float(CHIPS * CAP))
    src_row = to_row(flat)
    S = lax.broadcasted_iota(i32, (NB, CHIPS * CAP), 1).astype(f32)
    ret = jnp.sum(jnp.where((flat == S) & (slot < float(CAP)) & out_row, w, 0.0), axis=0, keepdims=True)
    ret = jnp.clip(ret, 0.0, NB - 1.0)
    K = lax.broadcasted_iota(i32, (NB, 128), 1).astype(f32)
    own = (owner == mef) & (slot == K)
    gath = jnp.max(jnp.where(own, lidx, 0.0), axis=0, keepdims=True)
    dest = jnp.max(jnp.where(own & out_row, lidx, -1.0), axis=0, keepdims=True)
    tab[...] = jnp.zeros((8, 512), i32)
    tab[0:1, 0:NB] = src_row.astype(i32)
    tab[1:2, :] = ret.astype(i32)
    tab[2:3, 0:128] = gath.astype(i32)
    tab[3:4, 0:128] = dest.astype(i32)
    tab[4:5, 0:NB] = to_row(ts).astype(i32)
    tab[5:6, 0:NB] = to_row(w).astype(i32)
    tab[6:7, 0:128] = jnp.broadcast_to(jnp.where(flag, 1, 0), (1, 128)).astype(i32)
    copy = pltpu.make_async_copy(tab.at[2:3, 0:128], tab_s, sem)
    copy.start()
    copy.wait()
    copies = []
    for k in range(CAP):
        row = tab_s[0, k]
        copies.append(pltpu.make_async_copy(mat.at[pl.ds(row, 1), :], comp.at[pl.ds(k, 1), :], row_sems.at[k]))
    for copy in copies:
        copy.start()
    for copy in copies:
        copy.wait()


def plan(pivots, matrix):
    vm = pl.BlockSpec(memory_space=pltpu.VMEM)
    return pl.pallas_call(
        plan_kernel,
        out_shape=(jax.ShapeDtypeStruct((8, 512), i32), jax.ShapeDtypeStruct((CAP, COLS), f32)),
        in_specs=[vm, pl.BlockSpec(memory_space=pl.ANY)],
        out_specs=(vm, vm),
        scratch_shapes=[
            pltpu.SMEM((1, 128), i32),
            pltpu.SemaphoreType.DMA,
            pltpu.SemaphoreType.DMA((CAP,)),
        ],
        compiler_params=pltpu.CompilerParams(vmem_limit_bytes=16 << 20),
        name="plan",
    )(pivots.reshape(1, NB), matrix)


def move_kernel(tab, comp, mat, lp, inv, u, sw, lg, nr, top, psib, invf, orig, ret,
                s_nr, r_nr, s_or, r_or, s_y, r_inv, r_lp, s_sib, r_psib, r_osib, s_ret, r_ret, s_ring, r_tile, r_usib,
                relay, s_relay, r_relay):
    me = lax.axis_index("prow")
    yy = lax.axis_index("pcol")
    core = me % 2
    chip = me // 2
    x = chip // NZ
    z = chip % NZ

    def tile_of(xx, zz):
        return (zz + NZ - 1) % NZ * NX + (xx + NX - 1) % NX

    def at(xx, zz, cc):
        return {"prow": (xx * NZ + zz) * 2 + cc, "pcol": yy}

    def peer(dchip):
        return {"prow": dchip * 2 + core, "pcol": yy}

    my_half = pl.ds(pl.multiple_of(core * BLOCK, BLOCK), BLOCK)
    other_half = pl.ds(pl.multiple_of((1 - core) * BLOCK, BLOCK), BLOCK)
    sibling = at(x, z, 1 - core)
    jt = tile_of(x, z)
    holder = jt < TILES

    def remote(src, dst, ss, rs, dev):
        return pltpu.make_async_remote_copy(src_ref=src, dst_ref=dst, send_sem=ss, recv_sem=rs, device_id=dev, device_id_type=MESH)

    def drain(ref, sem):
        pltpu.make_async_copy(ref, ref, sem).wait()

    barrier = pltpu.get_barrier_semaphore()

    def greet(k, _):
        pl.semaphore_signal(barrier, inc=1, device_id=peer((chip + k) % CHIPS), device_id_type=MESH)
        return 0

    lax.fori_loop(1, CHIPS, greet, 0)
    pl.semaphore_signal(barrier, inc=1, device_id=sibling, device_id_type=MESH)
    for k in range(1, NY):
        pl.semaphore_signal(barrier, inc=1, device_id={"prow": me, "pcol": (yy + k) % NY}, device_id_type=MESH)
    pl.semaphore_wait(barrier, CHIPS - 1 + 1 + NY - 1)

    for k in range(1, NY):
        remote(inv, invf.at[yy], s_y.at[0], r_inv, {"prow": me, "pcol": (yy + k) % NY}).start()
    pltpu.make_async_copy(inv, invf.at[yy], r_inv).start()

    def spread(k):
        k = k * 13 % CHIPS
        return (x + k // NZ) % NX * NZ + (z + k) % NZ

    def send_new(k, _):
        d = spread(k)
        j = tile_of(d // NZ, d % NZ)

        @pl.when(j < TILES)
        def _():
            remote(
                comp.at[:, pl.ds(pl.multiple_of(j * 128, 128), 128)],
                nr.at[pl.ds(pl.multiple_of(chip * CAP, CAP), CAP), :],
                s_nr, r_nr, peer(d),
            ).start()

        return 0

    lax.fori_loop(1, CHIPS, send_new, 0)

    @pl.when(holder)
    def _():
        pltpu.make_async_copy(
            comp.at[:, pl.ds(pl.multiple_of(jt * 128, 128), 128)],
            nr.at[pl.ds(pl.multiple_of(chip * CAP, CAP), CAP), :],
            r_nr,
        ).start()

    @pl.when(chip == 0)
    def _():
        def send_orig(xx, zz, dst, sem, to):
            cols = pl.ds(tile_of(xx, zz) * 128, 128)
            remote(mat.at[pl.ds(0, BLOCK), cols], dst, s_or, sem, to).start()

        mine = orig.at[my_half, :]
        send_orig(1, 0, mine, r_or, at(1, 0, core))
        send_orig(2, 0, relay.at[0], r_relay.at[0], at(3, 0, core))
        for zz in AWAY:
            send_orig(1, zz, relay.at[zz], r_relay.at[zz], at(1, 0, core))
            send_orig(3, zz, relay.at[zz], r_relay.at[zz], at(3, 0, core))
            send_orig(2, zz, mine, r_or, at(2, zz, core))
        for zz in AWAY:
            send_orig(0, zz, mine, r_or, at(0, zz, core))

    for k in range(1, NY):
        remote(lp, lg.at[yy], s_y.at[1], r_lp, {"prow": me, "pcol": (yy + k) % NY}).start()
    pltpu.make_async_copy(lp, lg.at[yy], r_lp).start()

    nr[pl.ds(CHIPS * CAP, 8), :] = jnp.zeros((8, 128), f32)


    drain(invf, r_inv)

    @pl.when(holder)
    def _():
        drain(nr.at[pl.ds(0, CHIPS * CAP), :], r_nr)

        def arrange(b, _):
            for t in range(8):
                i = b * 8 + t
                top[pl.ds(i, 1), :] = nr[pl.ds(tab[0, i], 1), :]
            return 0

        lax.fori_loop(0, NB // 8, arrange, 0)
        full = invf[...].reshape(NB, NB)
        top[...] = jnp.dot(full, top[...], precision=lax.Precision.HIGHEST, preferred_element_type=f32)
        back = remote(top.at[other_half, :], psib, s_sib.at[0], r_psib, sibling)
        back.start()
        back.wait()
        u[jt, my_half, :] = top[my_half, :] + psib[...]

    @pl.when(jnp.logical_not(holder))
    def _():
        u[jt, my_half, :] = jnp.zeros((BLOCK, 128), f32)

    def rows_of(part):
        if part is None:
            return my_half
        return pl.ds(pl.multiple_of(core * BLOCK + part * 64, 64), 64)

    def push(xx, zz, part, tx, tz):
        j = tile_of(xx, zz)
        ref = u.at[j, rows_of(part), :]
        remote(ref, ref, s_ring, r_tile.at[j], at(tx, tz, core)).start()

    def share(xx, zz):
        j = tile_of(xx, zz)
        ref = u.at[j, my_half, :]
        remote(ref, ref, s_sib.at[1], r_usib, sibling).start()

    def arrived(xx, zz):
        j = tile_of(xx, zz)
        drain(u.at[j, my_half, :], r_tile.at[j])

    xp, xm, xf = (x + 1) % NX, (x + NX - 1) % NX, (x + 2) % NX
    zp, zm = (z + 1) % NZ, (z + NZ - 1) % NZ

    def give_back():
        @pl.when(holder)
        def _():
            drain(orig.at[my_half, :], r_or)
            ref = orig.at[my_half, :]
            copy = remote(ref, ref, s_sib.at[2], r_osib, sibling)
            copy.start()
            copy.wait()

            def arrange(b, _):
                for t in range(8):
                    i = b * 8 + t
                    ret[pl.ds(i, 1), :] = orig[pl.ds(tab[1, i], 1), :]
                return 0

            lax.fori_loop(0, CHIPS * CAP // 8, arrange, 0)

            def send(k, _):
                d = spread(k)
                remote(ret.at[pl.ds(pl.multiple_of(d * CAP, CAP), CAP), :], sw.at[jt], s_ret, r_ret, peer(d)).start()
                return 0

            lax.fori_loop(1, CHIPS, send, 0)
            pltpu.make_async_copy(ret.at[pl.ds(pl.multiple_of(chip * CAP, CAP), CAP), :], sw.at[jt], r_ret).start()

    def x_neighbours(zz):
        arrived(xm, zz)
        push(xm, zz, 0, xp, z)
        share(xm, zz)
        arrived(xp, zz)
        push(xp, zz, 1, xm, z)
        share(xp, zz)

    def x_far(zz):
        arrived(xf, zz)
        share(xf, zz)

    def z_step(xx, s):
        for sign in (1, -1):
            zz = (z - sign * s + NZ) % NZ
            if s == NZ // 2 and sign == -1:
                continue
            arrived(xx, zz)
            if s < NZ // 2 - 1:
                push(xx, zz, None, x, (z + sign + NZ) % NZ)
            elif s == NZ // 2 - 1:
                push(xx, zz, 0 if sign == 1 else 1, x, (z + sign + NZ) % NZ)
            share(xx, zz)

    push(x, z, None, x, zp)
    push(x, z, None, x, zm)
    push(x, z, None, xp, z)
    push(x, z, None, xm, z)

    @pl.when(core == 0)
    def _():
        push(x, z, None, x, (z + 2) % NZ)
        push(x, z, None, x, (z + NZ - 2) % NZ)

    @pl.when(core == 1)
    def _():
        push(x, z, None, xf, z)

    share(x, z)

    def hand_on(zz):
        @pl.when((z == 0) & ((x == 3) | ((x == 1) & (zz > 0))))
        def _():
            drain(relay.at[zz], r_relay.at[zz])
            to = at(x, zz, core) if zz > 0 else at(2, 0, core)
            remote(relay.at[zz], orig.at[my_half, :], s_relay, r_or, to).start()

    hand_on(0)
    for zz in AWAY[:3]:
        hand_on(zz)

    def back(s):
        return (z + NZ - s) % NZ

    def onward(zz):
        push(x, zz, None, xp, z)
        push(x, zz, None, xm, z)
        share(x, zz)

    @pl.when(core == 0)
    def _():
        for s in (2, -2):
            arrived(x, back(s))
            push(x, back(s), None, x, back(-s // 2))
            push(x, back(s), 0 if s > 0 else 1, x, back(-s))
            onward(back(s))
        for s in (1, -1):
            arrived(x, back(s))
            onward(back(s))
        for zz in AWAY[3:]:
            hand_on(zz)
        x_neighbours(z)
        for s in (3, -3):
            arrived(x, back(s))
            onward(back(s))
        for s in (2, -2):
            x_neighbours(back(s))
        arrived(x, back(4))
        onward(back(4))
        give_back()
        for s in (1, -1):
            x_neighbours(back(s))
        x_far(z)
        for s in (3, -3):
            x_neighbours(back(s))
        for s in (2, -2, 1, -1):
            x_far(back(s))
        x_neighbours(back(4))
        for s in (3, -3, 4):
            x_far(back(s))

    @pl.when(core == 1)
    def _():
        for xx in (xm, xp, xf):
            arrived(xx, z)
            push(xx, z, None, x, zp)
            push(xx, z, None, x, zm)
            share(xx, z)
        for zz in AWAY[3:]:
            hand_on(zz)
        for s in range(1, NZ // 2 + 1):
            for xx in (x, xm, xp, xf):
                z_step(xx, s)
            if s == 1:
                give_back()

    drain(lg, r_lp)
    drain(sw.at[pl.ds(0, TILES)], r_ret)
    drain(u.at[pl.ds(0, CHIPS), other_half, :], r_usib)
    drain(u.at[pl.ds(0, CHIPS), my_half, :], s_sib.at[1])
    drain(u.at[pl.ds(0, CHIPS - 1), my_half, :], s_ring)
    drain(invf.at[pl.ds(0, NY - 1)], s_y.at[0])
    drain(lg.at[pl.ds(0, NY - 1)], s_y.at[1])

    @pl.when(holder)
    def _():
        drain(nr.at[pl.ds(0, (TILES - 1) * CAP), :], s_nr)
        drain(ret.at[pl.ds(0, (CHIPS - 1) * CAP), :], s_ret)

    @pl.when(jnp.logical_not(holder))
    def _():
        drain(nr.at[pl.ds(0, TILES * CAP), :], s_nr)

    @pl.when((z == 0) & (x == 1))
    def _():
        drain(relay.at[pl.ds(1, NZ - 1)], s_relay)

    @pl.when((z == 0) & (x == 3))
    def _():
        drain(relay, s_relay)

    @pl.when(chip == 0)
    def _():
        drain(mat.at[pl.ds(0, BLOCK), :], s_or)


def move(tab, comp, matrix, lower_panel, inverse):
    vm = pl.BlockSpec(memory_space=pltpu.VMEM)
    dma = pltpu.SemaphoreType.DMA
    return pl.pallas_call(
        move_kernel,
        out_shape=(
            jax.ShapeDtypeStruct((CHIPS, NB, 128), f32),
            jax.ShapeDtypeStruct((CHIPS, CAP, 128), f32),
            jax.ShapeDtypeStruct((NY, ROWS // NY, NB), f32),
        ),
        in_specs=[pl.BlockSpec(memory_space=pltpu.SMEM), vm, pl.BlockSpec(memory_space=pl.ANY), vm, vm],
        out_specs=(vm, vm, vm),
        scratch_shapes=[
            pltpu.VMEM((CHIPS * CAP + 8, 128), f32),
            pltpu.VMEM((NB, 128), f32),
            pltpu.VMEM((BLOCK, 128), f32),
            pltpu.VMEM((NY, NB // NY, NB), f32),
            pltpu.VMEM((NB, 128), f32),
            pltpu.VMEM((CHIPS * CAP, 128), f32),
            dma, dma, dma, dma, dma((2,)), dma, dma, dma((3,)), dma, dma, dma, dma, dma, dma((CHIPS,)), dma,
            pltpu.VMEM((NZ, BLOCK, 128), f32), dma, dma((NZ,)),
        ],
        compiler_params=pltpu.CompilerParams(collective_id=0, has_side_effects=True, vmem_limit_bytes=16 << 20),
        name="move",
    )(tab, comp, matrix, lower_panel, inverse)


def split(v):
    hi = v.astype(bf16)
    return hi, (v - hi.astype(f32)).astype(bf16)


def update_kernel(tab, mat, u, sw, lg, out, l_hi, l_lo, lu):
    me = lax.axis_index("prow")

    @pl.when(pl.program_id(0) == 0)
    def _():
        hi, lo = split(lg[...])
        l_hi[...] = hi
        l_lo[...] = lo

    uu = jnp.concatenate([u[k] for k in range(NX)], axis=1)
    u_hi, u_lo = split(uu)
    prod = functools.partial(jnp.dot, preferred_element_type=f32)
    lu[...] = prod(l_hi[...], u_hi) + (prod(l_lo[...], u_hi) + prod(l_hi[...], u_lo))
    out[...] = mat[...] - lu[...]
    for k in range(CAP):
        row = tab[3, k]

        @pl.when(row >= 0)
        def _():
            new = jnp.concatenate([sw[t, k : k + 1, :] for t in range(NX)], axis=1)
            out[pl.ds(row, 1), :] = new - lu[pl.ds(row, 1), :]

    for half in range(2):

        @pl.when(me == half)
        def _():
            out[0:BLOCK, :] = jnp.concatenate([u[k, half * BLOCK : (half + 1) * BLOCK, :] for k in range(NX)], axis=1)


def update(tab, matrix, u, sw, lg):
    width = NX * 128
    return pl.pallas_call(
        update_kernel,
        grid=(NZ,),
        out_shape=jax.ShapeDtypeStruct((ROWS, COLS), f32),
        in_specs=[
            pl.BlockSpec(memory_space=pltpu.SMEM),
            pl.BlockSpec((ROWS, width), lambda g: (0, g)),
            pl.BlockSpec((NX, NB, 128), lambda g: (g, 0, 0)),
            pl.BlockSpec((NX, CAP, 128), lambda g: (g, 0, 0)),
            pl.BlockSpec((ROWS, NB), lambda g: (0, 0)),
        ],
        out_specs=pl.BlockSpec((ROWS, width), lambda g: (0, g)),
        scratch_shapes=[pltpu.VMEM((ROWS, NB), bf16), pltpu.VMEM((ROWS, NB), bf16), pltpu.VMEM((ROWS, width), f32)],
        compiler_params=pltpu.CompilerParams(vmem_limit_bytes=16 << 20),
        name="update",
    )(tab, matrix, u, sw, lg)


def total(value, axis, size):
    step = 1
    while step < size:
        value = value + lax.ppermute(value, axis, [(i, i ^ step) for i in range(size)])
        step *= 2
    return value


def general(matrix, lg, inverse, source, moved):
    my_row = lax.axis_index("prow")
    row_count = lax.axis_size("prow")
    high = functools.partial(jnp.dot, precision=lax.Precision.HIGHEST, preferred_element_type=f32)
    local_rows = jnp.arange(ROWS, dtype=i32)
    global_rows = (local_rows // BLOCK * row_count + my_row) * BLOCK + local_rows % BLOCK
    owner = source // BLOCK % row_count
    local_index = source // BLOCK // row_count * BLOCK + source % BLOCK
    new_part = jnp.where((owner == my_row)[:, None], jnp.take(matrix, local_index, axis=0), 0.0)
    block_ids = jnp.arange(NB // BLOCK, dtype=i32)
    orig_part = jnp.where((block_ids == my_row)[:, None, None], matrix[None, :BLOCK], 0.0).reshape(NB, COLS)
    gathered, top_orig = jnp.split(total(jnp.concatenate([new_part, orig_part]), "prow", N_PROW), 2)
    hit = (source[None, :] == global_rows[:, None]) & (global_rows >= NB)[:, None]
    fetch = jnp.max(jnp.where(hit, moved[None, :], -1), axis=1)
    swapped = jnp.where((fetch >= 0)[:, None], jnp.take(top_orig, jnp.clip(fetch, 0, NB - 1), axis=0), matrix)
    parts = jnp.where((jnp.arange(NY) == lax.axis_index("pcol"))[:, None, None], inverse[None], 0.0)
    u_rows = high(total(parts.reshape(NB, NB), "pcol", NY), gathered)
    result = swapped - high(lg, u_rows)
    head = lax.dynamic_slice_in_dim(u_rows, jnp.minimum(my_row, 1) * BLOCK, BLOCK, 0)
    first = jnp.where(my_row < 2, head, result[:BLOCK])
    return jnp.concatenate([first, result[BLOCK:]], axis=0)


def local(matrix, lower_panel, inverse, pivots):
    tab, comp = plan(pivots, matrix)
    u, sw, lg = move(tab, comp, matrix, lower_panel, inverse)
    lg = lg.reshape(ROWS, NB)
    result = update(tab, matrix, u, sw, lg)
    _, result = lax.while_loop(
        lambda state: state[0] > 0,
        lambda state: (jnp.int32(0), general(matrix, lg, inverse, tab[4, :NB], tab[5, :NB])),
        (tab[6, 0], result),
    )
    return result


def solution(mesh):
    return jax.shard_map(
        local,
        mesh=mesh,
        in_specs=(P("prow", "pcol"), P(("prow", "pcol"), None), P("pcol", None), P()),
        out_specs=P("prow", "pcol"),
        check_vma=False,
    )
```

```python
import functools

import jax
import jax.numpy as jnp
from jax import lax
from jax.experimental import pallas as pl
from jax.experimental.pallas import tpu as pltpu
from jax.sharding import PartitionSpec as P

BLOCK = 128
NB = 256
CAP = 16
NX, NZ, NY = 4, 8, 4
N_PROW = 64
CHIPS = NX * NZ
STEP = 10
SHARE = ((0, 112), (112, 144))
AWAY = (4, 3, 5, 2, 6, 1, 7)
TILES = 30
COLS = TILES * 128
ROWS = 384
MESH = pl.DeviceIdType.MESH
f32 = jnp.float32
i32 = jnp.int32
bf16 = jnp.bfloat16


def plan_kernel(p_ref, mat, tab, comp, crowded, tab_s, sem, row_sems):
    me = lax.axis_index("prow")
    core = (me % 2).astype(f32)
    mef = me.astype(f32)
    big = (NB, NB)
    I = lax.broadcasted_iota(i32, big, 0)
    J = lax.broadcasted_iota(i32, big, 1)
    Jf = J.astype(f32)
    eye = I == J
    lt = J < I
    PB = jnp.broadcast_to(p_ref[...].astype(f32), big)

    def to_col(row_b):
        return jnp.sum(jnp.where(eye, row_b, 0.0), axis=1, keepdims=True)

    def to_row(col):
        return jnp.sum(jnp.where(eye, jnp.broadcast_to(col, big), 0.0), axis=0, keepdims=True)

    def pick(col_idx, row_vals):
        return jnp.sum(jnp.where(Jf == col_idx, jnp.broadcast_to(row_vals, big), 0.0), axis=1, keepdims=True)

    p_col = to_col(PB)
    eq = (p_col == PB) & lt
    prev = jnp.max(jnp.where(eq, Jf, -1.0), axis=1, keepdims=True)
    later = jnp.max(jnp.where(eq, 1.0, 0.0), axis=0, keepdims=True)
    par = jnp.max(jnp.where((PB == I.astype(f32)) & lt, Jf, -1.0), axis=1, keepdims=True)
    icol = lax.broadcasted_iota(i32, (NB, 1), 0).astype(f32)
    root = jnp.where(par < 0.0, icol, par)

    def more(state):
        return state[1] > 0.0

    def double(state):
        r, _ = state
        nr = pick(r, to_row(r))
        return nr, jnp.max(r - nr)

    root, _ = lax.while_loop(more, double, (root, jnp.float32(1.0)))
    c_row = to_row(root)
    ts = jnp.where(prev >= 0.0, pick(prev, c_row), p_col)
    tsi = ts.astype(i32)
    owner_i = lax.shift_right_logical(tsi, 7) & 63
    owner = owner_i.astype(f32)
    lidx = (lax.shift_right_logical(tsi, 13) * BLOCK + (tsi & 127)).astype(f32)
    slot = jnp.sum(jnp.where((owner == jnp.broadcast_to(to_row(owner), big)) & lt, 1.0, 0.0), axis=1, keepdims=True)
    last_c = jnp.broadcast_to(jnp.where(later > 0.0, 0.0, c_row), big)
    w = jnp.sum(jnp.where(ts == PB, last_c, 0.0), axis=1, keepdims=True)
    out_row = ts >= float(NB)
    flag = jnp.max(slot) >= float(CAP)
    mine_core = (owner_i & 1).astype(f32) == core
    chip = lax.shift_right_logical(owner_i, 1).astype(f32)
    flat = jnp.where(mine_core, chip * CAP + slot, float(CHIPS * CAP))
    flat = jnp.minimum(flat, float(CHIPS * CAP))
    src_row = to_row(flat)
    S = lax.broadcasted_iota(i32, (NB, CHIPS * CAP), 1).astype(f32)
    ret = jnp.sum(jnp.where((flat == S) & (slot < float(CAP)) & out_row, w, 0.0), axis=0, keepdims=True)
    ret = jnp.clip(ret, 0.0, NB - 1.0)
    K = lax.broadcasted_iota(i32, (NB, 128), 1).astype(f32)
    own = (owner == mef) & (slot == K)
    gath = jnp.max(jnp.where(own, lidx, 0.0), axis=0, keepdims=True)
    dest = jnp.max(jnp.where(own & out_row, lidx, -1.0), axis=0, keepdims=True)
    tab[...] = jnp.zeros((8, 512), i32)
    tab[0:1, 0:NB] = src_row.astype(i32)
    tab[1:2, :] = ret.astype(i32)
    tab[2:3, 0:128] = gath.astype(i32)
    tab[3:4, 0:128] = dest.astype(i32)
    tab[4:5, 0:NB] = to_row(ts).astype(i32)
    tab[5:6, 0:NB] = to_row(w).astype(i32)
    crowded[0, 0] = jnp.where(flag, 1, 0)
    copy = pltpu.make_async_copy(tab.at[2:3, 0:128], tab_s, sem)
    copy.start()
    copy.wait()
    copies = []
    for k in range(CAP):
        row = tab_s[0, k]
        copies.append(pltpu.make_async_copy(mat.at[pl.ds(row, 1), :], comp.at[pl.ds(k, 1), :], row_sems.at[k]))
    for copy in copies:
        copy.start()
    for copy in copies:
        copy.wait()


def plan(pivots, matrix):
    vm = pl.BlockSpec(memory_space=pltpu.VMEM)
    return pl.pallas_call(
        plan_kernel,
        out_shape=(
            jax.ShapeDtypeStruct((8, 512), i32),
            jax.ShapeDtypeStruct((CAP, COLS), f32),
            jax.ShapeDtypeStruct((1, 1), i32),
        ),
        in_specs=[vm, pl.BlockSpec(memory_space=pl.ANY)],
        out_specs=(vm, vm, pl.BlockSpec(memory_space=pltpu.SMEM)),
        scratch_shapes=[
            pltpu.SMEM((1, 128), i32),
            pltpu.SemaphoreType.DMA,
            pltpu.SemaphoreType.DMA((CAP,)),
        ],
        compiler_params=pltpu.CompilerParams(vmem_limit_bytes=16 << 20),
        name="plan",
    )(pivots.reshape(1, NB), matrix)


def move_kernel(tab, comp, mat, lp, inv, u, sw, lg, nr, top, psib, invf, orig, ret,
                s_nr, r_nr, s_or, r_or, s_y, r_inv, r_lp, s_sib, r_psib, r_osib, s_ret, r_ret, s_ring, r_tile, r_usib,
                relay, s_relay, r_relay):
    me = lax.axis_index("prow")
    yy = lax.axis_index("pcol")
    core = me % 2
    chip = me // 2
    x = chip // NZ
    z = chip % NZ

    def tile_of(xx, zz):
        return (zz + NZ - 1) % NZ * NX + (xx + NX - 1) % NX

    def at(xx, zz, cc):
        return {"prow": (xx * NZ + zz) * 2 + cc, "pcol": yy}

    def peer(dchip):
        return {"prow": dchip * 2 + core, "pcol": yy}

    my_half = pl.ds(pl.multiple_of(core * BLOCK, BLOCK), BLOCK)
    sibling = at(x, z, 1 - core)
    jt = tile_of(x, z)
    holder = jt < TILES

    def remote(src, dst, ss, rs, dev):
        return pltpu.make_async_remote_copy(src_ref=src, dst_ref=dst, send_sem=ss, recv_sem=rs, device_id=dev, device_id_type=MESH)

    def drain(ref, sem):
        pltpu.make_async_copy(ref, ref, sem).wait()

    barrier = pltpu.get_barrier_semaphore()

    def greet(k, _):
        pl.semaphore_signal(barrier, inc=1, device_id=peer((chip + k) % CHIPS), device_id_type=MESH)
        return 0

    lax.fori_loop(1, CHIPS, greet, 0)
    pl.semaphore_signal(barrier, inc=1, device_id=sibling, device_id_type=MESH)
    for k in range(1, NY):
        pl.semaphore_signal(barrier, inc=1, device_id={"prow": me, "pcol": (yy + k) % NY}, device_id_type=MESH)
    pl.semaphore_wait(barrier, CHIPS - 1 + 1 + NY - 1)

    for k in range(1, NY):
        remote(inv, invf.at[yy], s_y.at[0], r_inv, {"prow": me, "pcol": (yy + k) % NY}).start()
    pltpu.make_async_copy(inv, invf.at[yy], r_inv).start()

    def spread(k):
        k = k * 13 % CHIPS
        return (x + k // NZ) % NX * NZ + (z + k) % NZ

    def send_new(k, _):
        d = spread(k)
        j = tile_of(d // NZ, d % NZ)

        @pl.when(j < TILES)
        def _():
            remote(
                comp.at[:, pl.ds(pl.multiple_of(j * 128, 128), 128)],
                nr.at[pl.ds(pl.multiple_of(chip * CAP, CAP), CAP), :],
                s_nr, r_nr, peer(d),
            ).start()

        return 0

    lax.fori_loop(1, CHIPS, send_new, 0)

    @pl.when(holder)
    def _():
        pltpu.make_async_copy(
            comp.at[:, pl.ds(pl.multiple_of(jt * 128, 128), 128)],
            nr.at[pl.ds(pl.multiple_of(chip * CAP, CAP), CAP), :],
            r_nr,
        ).start()

    @pl.when(chip == 0)
    def _():
        def send_orig(xx, zz, dst, sem, to):
            cols = pl.ds(tile_of(xx, zz) * 128, 128)
            remote(mat.at[pl.ds(0, BLOCK), cols], dst, s_or, sem, to).start()

        mine = orig.at[my_half, :]
        send_orig(1, 0, mine, r_or, at(1, 0, core))
        send_orig(2, 0, relay.at[0], r_relay.at[0], at(3, 0, core))
        for zz in AWAY:
            send_orig(1, zz, relay.at[zz], r_relay.at[zz], at(1, 0, core))
            send_orig(3, zz, relay.at[zz], r_relay.at[zz], at(3, 0, core))
            send_orig(2, zz, mine, r_or, at(2, zz, core))
        for zz in AWAY:
            send_orig(0, zz, mine, r_or, at(0, zz, core))

    for k in range(1, NY):
        remote(lp, lg.at[yy], s_y.at[1], r_lp, {"prow": me, "pcol": (yy + k) % NY}).start()
    pltpu.make_async_copy(lp, lg.at[yy], r_lp).start()

    nr[pl.ds(CHIPS * CAP, 8), :] = jnp.zeros((8, 128), f32)


    drain(invf, r_inv)

    @pl.when(holder)
    def _():
        drain(nr.at[pl.ds(0, CHIPS * CAP), :], r_nr)

        def arrange(b, _):
            for t in range(8):
                i = b * 8 + t
                top[pl.ds(i, 1), :] = nr[pl.ds(tab[0, i], 1), :]
            return 0

        lax.fori_loop(0, NB // 8, arrange, 0)
        full = invf[...].reshape(NB, NB)
        top[...] = jnp.dot(full, top[...], precision=lax.Precision.HIGHEST, preferred_element_type=f32)

        def finish(c):
            own, other = (pl.ds(*SHARE[c]), pl.ds(*SHARE[1 - c]))
            part = psib.at[pl.ds(0, SHARE[c][1])]
            out = remote(top.at[other], psib.at[pl.ds(0, SHARE[1 - c][1])], s_sib.at[0], r_psib, sibling)
            out.start()
            drain(part, r_psib)
            u[jt, own, :] = top[own, :] + part[...]
            out.wait_send()

        pl.when(core == 0)(lambda: finish(0))
        pl.when(core == 1)(lambda: finish(1))

    for c in range(2):

        @pl.when(jnp.logical_not(holder) & (core == c))
        def _():
            u[jt, pl.ds(*SHARE[c]), :] = jnp.zeros((SHARE[c][1], 128), f32)

    def rows_of(c, part=None):
        start, size = SHARE[c]
        return pl.ds(start, size) if part is None else pl.ds(start + part * (size // 2), size // 2)

    def push(c, xx, zz, part, tx, tz):
        j = tile_of(xx, zz)
        ref = u.at[j, rows_of(c, part), :]
        remote(ref, ref, s_ring, r_tile.at[j], at(tx, tz, core)).start()

    def share(c, xx, zz):
        j = tile_of(xx, zz)
        ref = u.at[j, rows_of(c), :]
        remote(ref, ref, s_sib.at[1], r_usib, sibling).start()

    def arrived(c, xx, zz):
        j = tile_of(xx, zz)
        drain(u.at[j, rows_of(c), :], r_tile.at[j])

    xp, xm, xf = (x + 1) % NX, (x + NX - 1) % NX, (x + 2) % NX
    zp, zm = (z + 1) % NZ, (z + NZ - 1) % NZ

    def swap_halves():
        ref = orig.at[my_half, :]
        return remote(ref, ref, s_sib.at[2], r_osib, sibling)

    def swap_first():
        @pl.when(holder)
        def _():
            drain(orig.at[my_half, :], r_or)
            swap_halves().start()

    def give_back():
        @pl.when(holder)
        def _():
            swap_halves().wait()

            def arrange(b, _):
                for t in range(8):
                    i = b * 8 + t
                    ret[pl.ds(i, 1), :] = orig[pl.ds(tab[1, i], 1), :]
                return 0

            lax.fori_loop(0, CHIPS * CAP // 8, arrange, 0)

            def send(k, _):
                d = spread(k)
                remote(ret.at[pl.ds(pl.multiple_of(d * CAP, CAP), CAP), :], sw.at[jt], s_ret, r_ret, peer(d)).start()
                return 0

            lax.fori_loop(1, CHIPS, send, 0)
            pltpu.make_async_copy(ret.at[pl.ds(pl.multiple_of(chip * CAP, CAP), CAP), :], sw.at[jt], r_ret).start()

    def x_neighbours(zz):
        arrived(0, xm, zz)
        push(0, xm, zz, 0, xp, z)
        share(0, xm, zz)
        arrived(0, xp, zz)
        push(0, xp, zz, 1, xm, z)
        share(0, xp, zz)

    def x_far(zz):
        arrived(0, xf, zz)
        share(0, xf, zz)

    def z_step(xx, s):
        for sign in (1, -1):
            zz = (z - sign * s + NZ) % NZ
            if s == NZ // 2 and sign == -1:
                continue
            arrived(1, xx, zz)
            if s < NZ // 2 - 1:
                push(1, xx, zz, None, x, (z + sign + NZ) % NZ)
            elif s == NZ // 2 - 1:
                push(1, xx, zz, 0 if sign == 1 else 1, x, (z + sign + NZ) % NZ)
            share(1, xx, zz)

    def begin(c):
        push(c, x, z, None, x, zp)
        push(c, x, z, None, x, zm)
        push(c, x, z, None, xp, z)
        push(c, x, z, None, xm, z)
        if c == 0:
            push(c, x, z, None, x, (z + 2) % NZ)
            push(c, x, z, None, x, (z + NZ - 2) % NZ)
        else:
            push(c, x, z, None, xf, z)
        share(c, x, z)

    pl.when(core == 0)(lambda: begin(0))
    pl.when(core == 1)(lambda: begin(1))

    def hand_on(zz):
        @pl.when((z == 0) & ((x == 3) | ((x == 1) & (zz > 0))))
        def _():
            drain(relay.at[zz], r_relay.at[zz])
            to = at(x, zz, core) if zz > 0 else at(2, 0, core)
            remote(relay.at[zz], orig.at[my_half, :], s_relay, r_or, to).start()

    hand_on(0)
    for zz in AWAY[:3]:
        hand_on(zz)

    def back(s):
        return (z + NZ - s) % NZ

    def onward(zz):
        push(0, x, zz, None, xp, z)
        push(0, x, zz, None, xm, z)
        share(0, x, zz)

    @pl.when(core == 0)
    def _():
        for s in (2, -2):
            arrived(0, x, back(s))
            push(0, x, back(s), None, x, back(-s // 2))
            push(0, x, back(s), 0 if s > 0 else 1, x, back(-s))
            onward(back(s))
        for s in (1, -1):
            arrived(0, x, back(s))
            onward(back(s))
        for zz in AWAY[3:]:
            hand_on(zz)
        x_neighbours(z)
        for s in (3, -3):
            arrived(0, x, back(s))
            onward(back(s))
        swap_first()
        for s in (2, -2):
            x_neighbours(back(s))
        arrived(0, x, back(4))
        onward(back(4))
        give_back()
        for s in (1, -1):
            x_neighbours(back(s))
        x_far(z)
        for s in (3, -3):
            x_neighbours(back(s))
        for s in (2, -2, 1, -1):
            x_far(back(s))
        x_neighbours(back(4))
        for s in (3, -3, 4):
            x_far(back(s))

    @pl.when(core == 1)
    def _():
        for xx in (xm, xp, xf):
            arrived(1, xx, z)
            push(1, xx, z, None, x, zp)
            push(1, xx, z, None, x, zm)
            share(1, xx, z)
        for zz in AWAY[3:]:
            hand_on(zz)
        for s in range(1, NZ // 2 + 1):
            for xx in (x, xm, xp, xf):
                z_step(xx, s)
            if s == 1:
                swap_first()
            if s == 2:
                give_back()

    drain(lg, r_lp)
    drain(sw.at[pl.ds(0, TILES)], r_ret)
    def end(c):
        drain(u.at[pl.ds(0, CHIPS), pl.ds(*SHARE[1 - c]), :], r_usib)
        drain(u.at[pl.ds(0, CHIPS), pl.ds(*SHARE[c]), :], s_sib.at[1])
        drain(u.at[pl.ds(0, CHIPS - 1), pl.ds(*SHARE[c]), :], s_ring)

    pl.when(core == 0)(lambda: end(0))
    pl.when(core == 1)(lambda: end(1))
    drain(invf.at[pl.ds(0, NY - 1)], s_y.at[0])
    drain(lg.at[pl.ds(0, NY - 1)], s_y.at[1])

    @pl.when(holder)
    def _():
        drain(nr.at[pl.ds(0, (TILES - 1) * CAP), :], s_nr)
        drain(ret.at[pl.ds(0, (CHIPS - 1) * CAP), :], s_ret)

    @pl.when(jnp.logical_not(holder))
    def _():
        drain(nr.at[pl.ds(0, TILES * CAP), :], s_nr)

    @pl.when((z == 0) & (x == 1))
    def _():
        drain(relay.at[pl.ds(1, NZ - 1)], s_relay)

    @pl.when((z == 0) & (x == 3))
    def _():
        drain(relay, s_relay)

    @pl.when(chip == 0)
    def _():
        drain(mat.at[pl.ds(0, BLOCK), :], s_or)


def move(tab, comp, matrix, lower_panel, inverse):
    vm = pl.BlockSpec(memory_space=pltpu.VMEM)
    dma = pltpu.SemaphoreType.DMA
    return pl.pallas_call(
        move_kernel,
        out_shape=(
            jax.ShapeDtypeStruct((CHIPS, NB, 128), f32),
            jax.ShapeDtypeStruct((CHIPS, CAP, 128), f32),
            jax.ShapeDtypeStruct((NY, ROWS // NY, NB), f32),
        ),
        in_specs=[pl.BlockSpec(memory_space=pltpu.SMEM), vm, pl.BlockSpec(memory_space=pl.ANY), vm, vm],
        out_specs=(vm, vm, vm),
        scratch_shapes=[
            pltpu.VMEM((CHIPS * CAP + 8, 128), f32),
            pltpu.VMEM((NB, 128), f32),
            pltpu.VMEM((max(SHARE[0][1], SHARE[1][1]), 128), f32),
            pltpu.VMEM((NY, NB // NY, NB), f32),
            pltpu.VMEM((NB, 128), f32),
            pltpu.VMEM((CHIPS * CAP, 128), f32),
            dma, dma, dma, dma, dma((2,)), dma, dma, dma((3,)), dma, dma, dma, dma, dma, dma((CHIPS,)), dma,
            pltpu.VMEM((NZ, BLOCK, 128), f32), dma, dma((NZ,)),
        ],
        compiler_params=pltpu.CompilerParams(collective_id=0, has_side_effects=True, vmem_limit_bytes=16 << 20),
        name="move",
    )(tab, comp, matrix, lower_panel, inverse)


def split(v):
    hi = v.astype(bf16)
    return hi, (v - hi.astype(f32)).astype(bf16)


def update_kernel(tab, mat, u, sw, lg, out, l_cat):
    me = lax.axis_index("prow")

    @pl.when(pl.program_id(0) == 0)
    def _():
        hi, lo = split(lg[...])
        l_cat[...] = jnp.concatenate([hi, lo, hi], axis=1)

    first = pl.program_id(0) * STEP
    cols = pl.ds(pl.multiple_of(first * 128, 128), STEP * 128)
    u_hi, u_lo = split(jnp.concatenate([u[first + k] for k in range(STEP)], axis=1))
    out[...] = mat[:, cols] - jnp.dot(l_cat[...], jnp.concatenate([u_hi, u_hi, u_lo], axis=0), preferred_element_type=f32)
    for k in range(CAP):
        row = tab[3, k]

        @pl.when(row >= 0)
        def _():
            new = jnp.concatenate([sw[first + t, k : k + 1, :] for t in range(STEP)], axis=1)
            out[pl.ds(row, 1), :] = out[pl.ds(row, 1), :] + (new - mat[pl.ds(row, 1), cols])

    for half in range(2):

        @pl.when(me == half)
        def _():
            for k in range(STEP):
                out[0:BLOCK, k * 128 : (k + 1) * 128] = u[first + k, half * BLOCK : (half + 1) * BLOCK, :]


def update(tab, matrix, u, sw, lg):
    vm = pl.BlockSpec(memory_space=pltpu.VMEM)
    return pl.pallas_call(
        update_kernel,
        grid=(TILES // STEP,),
        out_shape=jax.ShapeDtypeStruct((ROWS, COLS), f32),
        in_specs=[pl.BlockSpec(memory_space=pltpu.SMEM), vm, vm, vm, vm],
        out_specs=pl.BlockSpec((ROWS, STEP * 128), lambda g: (0, g)),
        scratch_shapes=[pltpu.VMEM((ROWS, 3 * NB), bf16)],
        compiler_params=pltpu.CompilerParams(vmem_limit_bytes=32 << 20),
        name="update",
    )(tab, matrix, u, sw, lg)


def total(value, axis, size):
    step = 1
    while step < size:
        value = value + lax.ppermute(value, axis, [(i, i ^ step) for i in range(size)])
        step *= 2
    return value


def general(matrix, lg, inverse, source, moved):
    my_row = lax.axis_index("prow")
    row_count = lax.axis_size("prow")
    high = functools.partial(jnp.dot, precision=lax.Precision.HIGHEST, preferred_element_type=f32)
    local_rows = jnp.arange(ROWS, dtype=i32)
    global_rows = (local_rows // BLOCK * row_count + my_row) * BLOCK + local_rows % BLOCK
    owner = source // BLOCK % row_count
    local_index = source // BLOCK // row_count * BLOCK + source % BLOCK
    new_part = jnp.where((owner == my_row)[:, None], jnp.take(matrix, local_index, axis=0), 0.0)
    block_ids = jnp.arange(NB // BLOCK, dtype=i32)
    orig_part = jnp.where((block_ids == my_row)[:, None, None], matrix[None, :BLOCK], 0.0).reshape(NB, COLS)
    gathered, top_orig = jnp.split(total(jnp.concatenate([new_part, orig_part]), "prow", N_PROW), 2)
    hit = (source[None, :] == global_rows[:, None]) & (global_rows >= NB)[:, None]
    fetch = jnp.max(jnp.where(hit, moved[None, :], -1), axis=1)
    swapped = jnp.where((fetch >= 0)[:, None], jnp.take(top_orig, jnp.clip(fetch, 0, NB - 1), axis=0), matrix)
    parts = jnp.where((jnp.arange(NY) == lax.axis_index("pcol"))[:, None, None], inverse[None], 0.0)
    u_rows = high(total(parts.reshape(NB, NB), "pcol", NY), gathered)
    result = swapped - high(lg, u_rows)
    head = lax.dynamic_slice_in_dim(u_rows, jnp.minimum(my_row, 1) * BLOCK, BLOCK, 0)
    first = jnp.where(my_row < 2, head, result[:BLOCK])
    return jnp.concatenate([first, result[BLOCK:]], axis=0)


def local(matrix, lower_panel, inverse, pivots):
    tab, comp, crowded = plan(pivots, matrix)
    u, sw, lg = move(tab, comp, matrix, lower_panel, inverse)
    lg = lg.reshape(ROWS, NB)
    result = update(tab, matrix, u, sw, lg)
    _, result = lax.while_loop(
        lambda state: state[0] > 0,
        lambda state: (jnp.int32(0), general(matrix, lg, inverse, tab[4, :NB], tab[5, :NB])),
        (crowded[0, 0], result),
    )
    return result


def solution(mesh):
    return jax.shard_map(
        local,
        mesh=mesh,
        in_specs=(P("prow", "pcol"), P(("prow", "pcol"), None), P("pcol", None), P()),
        out_specs=P("prow", "pcol"),
        check_vma=False,
    )
```

```python
import functools

import jax
import jax.numpy as jnp
from jax import lax
from jax.experimental import pallas as pl
from jax.experimental.pallas import tpu as pltpu
from jax.sharding import PartitionSpec as P

BLOCK = 128
NB = 256
CAP = 16
NX, NZ, NY = 4, 8, 4
N_PROW = 64
CHIPS = NX * NZ
STEP = 10
SHARE = ((0, 112), (112, 144))
AWAY = (4, 3, 5, 2, 6, 1, 7)
TILES = 30
COLS = TILES * 128
ROWS = 384
MESH = pl.DeviceIdType.MESH
f32 = jnp.float32
i32 = jnp.int32
bf16 = jnp.bfloat16


def plan_kernel(p_ref, mat, tab, comp, crowded, tab_s, sem, row_sems):
    me = lax.axis_index("prow")
    core = (me % 2).astype(f32)
    mef = me.astype(f32)
    big = (NB, NB)
    I = lax.broadcasted_iota(i32, big, 0)
    J = lax.broadcasted_iota(i32, big, 1)
    Jf = J.astype(f32)
    eye = I == J
    lt = J < I
    PB = jnp.broadcast_to(p_ref[...].astype(f32), big)

    def to_col(row_b):
        return jnp.sum(jnp.where(eye, row_b, 0.0), axis=1, keepdims=True)

    def to_row(col):
        return jnp.sum(jnp.where(eye, jnp.broadcast_to(col, big), 0.0), axis=0, keepdims=True)

    def pick(col_idx, row_vals):
        return jnp.sum(jnp.where(Jf == col_idx, jnp.broadcast_to(row_vals, big), 0.0), axis=1, keepdims=True)

    p_col = to_col(PB)
    eq = (p_col == PB) & lt
    prev = jnp.max(jnp.where(eq, Jf, -1.0), axis=1, keepdims=True)
    later = jnp.max(jnp.where(eq, 1.0, 0.0), axis=0, keepdims=True)
    par = jnp.max(jnp.where((PB == I.astype(f32)) & lt, Jf, -1.0), axis=1, keepdims=True)
    icol = lax.broadcasted_iota(i32, (NB, 1), 0).astype(f32)
    root = jnp.where(par < 0.0, icol, par)

    def more(state):
        return state[1] > 0.0

    def double(state):
        r, _ = state
        nr = pick(r, to_row(r))
        return nr, jnp.max(r - nr)

    root, _ = lax.while_loop(more, double, (root, jnp.float32(1.0)))
    c_row = to_row(root)
    ts = jnp.where(prev >= 0.0, pick(prev, c_row), p_col)
    tsi = ts.astype(i32)
    owner_i = lax.shift_right_logical(tsi, 7) & 63
    owner = owner_i.astype(f32)
    lidx = (lax.shift_right_logical(tsi, 13) * BLOCK + (tsi & 127)).astype(f32)
    slot = jnp.sum(jnp.where((owner == jnp.broadcast_to(to_row(owner), big)) & lt, 1.0, 0.0), axis=1, keepdims=True)
    last_c = jnp.broadcast_to(jnp.where(later > 0.0, 0.0, c_row), big)
    w = jnp.sum(jnp.where(ts == PB, last_c, 0.0), axis=1, keepdims=True)
    out_row = ts >= float(NB)
    flag = jnp.max(slot) >= float(CAP)
    mine_core = (owner_i & 1).astype(f32) == core
    chip = lax.shift_right_logical(owner_i, 1).astype(f32)
    flat = jnp.where(mine_core, chip * CAP + slot, float(CHIPS * CAP))
    flat = jnp.minimum(flat, float(CHIPS * CAP))
    src_row = to_row(flat)
    S = lax.broadcasted_iota(i32, (NB, CHIPS * CAP), 1).astype(f32)
    ret = jnp.sum(jnp.where((flat == S) & (slot < float(CAP)) & out_row, w, 0.0), axis=0, keepdims=True)
    ret = jnp.clip(ret, 0.0, NB - 1.0)
    K = lax.broadcasted_iota(i32, (NB, 128), 1).astype(f32)
    own = (owner == mef) & (slot == K)
    gath = jnp.max(jnp.where(own, lidx, 0.0), axis=0, keepdims=True)
    dest = jnp.max(jnp.where(own & out_row, lidx, -1.0), axis=0, keepdims=True)
    tab[...] = jnp.zeros((8, 512), i32)
    tab[0:1, 0:NB] = src_row.astype(i32)
    tab[1:2, :] = ret.astype(i32)
    tab[2:3, 0:128] = gath.astype(i32)
    tab[3:4, 0:128] = dest.astype(i32)
    tab[4:5, 0:NB] = to_row(ts).astype(i32)
    tab[5:6, 0:NB] = to_row(w).astype(i32)
    crowded[0, 0] = jnp.where(flag, 1, 0)
    copy = pltpu.make_async_copy(tab.at[2:3, 0:128], tab_s, sem)
    copy.start()
    copy.wait()
    copies = []
    for k in range(CAP):
        row = tab_s[0, k]
        copies.append(pltpu.make_async_copy(mat.at[pl.ds(row, 1), :], comp.at[pl.ds(k, 1), :], row_sems.at[k]))
    for copy in copies:
        copy.start()
    for copy in copies:
        copy.wait()


def plan(pivots, matrix):
    vm = pl.BlockSpec(memory_space=pltpu.VMEM)
    return pl.pallas_call(
        plan_kernel,
        out_shape=(
            jax.ShapeDtypeStruct((8, 512), i32),
            jax.ShapeDtypeStruct((CAP, COLS), f32),
            jax.ShapeDtypeStruct((1, 1), i32),
        ),
        in_specs=[vm, pl.BlockSpec(memory_space=pl.ANY)],
        out_specs=(vm, vm, pl.BlockSpec(memory_space=pltpu.SMEM)),
        scratch_shapes=[
            pltpu.SMEM((1, 128), i32),
            pltpu.SemaphoreType.DMA,
            pltpu.SemaphoreType.DMA((CAP,)),
        ],
        compiler_params=pltpu.CompilerParams(vmem_limit_bytes=16 << 20),
        name="plan",
    )(pivots.reshape(1, NB), matrix)


def move_kernel(tab, comp, mat, lp, inv, u, sw, lg, nr, top, psib, invf, orig, ret,
                s_nr, r_nr, s_or, r_or, s_y, r_inv, r_lp, s_sib, r_psib, r_osib, s_ret, r_ret, s_ring, r_tile, r_usib,
                relay, s_relay, r_relay, inv_cat):
    me = lax.axis_index("prow")
    yy = lax.axis_index("pcol")
    core = me % 2
    chip = me // 2
    x = chip // NZ
    z = chip % NZ

    def tile_of(xx, zz):
        return (zz + NZ - 1) % NZ * NX + (xx + NX - 1) % NX

    def at(xx, zz, cc):
        return {"prow": (xx * NZ + zz) * 2 + cc, "pcol": yy}

    def peer(dchip):
        return {"prow": dchip * 2 + core, "pcol": yy}

    my_half = pl.ds(pl.multiple_of(core * BLOCK, BLOCK), BLOCK)
    sibling = at(x, z, 1 - core)
    jt = tile_of(x, z)
    holder = jt < TILES

    def remote(src, dst, ss, rs, dev):
        return pltpu.make_async_remote_copy(src_ref=src, dst_ref=dst, send_sem=ss, recv_sem=rs, device_id=dev, device_id_type=MESH)

    def drain(ref, sem):
        pltpu.make_async_copy(ref, ref, sem).wait()

    barrier = pltpu.get_barrier_semaphore()

    def greet(k, _):
        pl.semaphore_signal(barrier, inc=1, device_id=peer((chip + k) % CHIPS), device_id_type=MESH)
        return 0

    lax.fori_loop(1, CHIPS, greet, 0)
    pl.semaphore_signal(barrier, inc=1, device_id=sibling, device_id_type=MESH)
    for k in range(1, NY):
        pl.semaphore_signal(barrier, inc=1, device_id={"prow": me, "pcol": (yy + k) % NY}, device_id_type=MESH)
    pl.semaphore_wait(barrier, CHIPS - 1 + 1 + NY - 1)

    for k in range(1, NY):
        remote(inv, invf.at[yy], s_y.at[0], r_inv, {"prow": me, "pcol": (yy + k) % NY}).start()
    pltpu.make_async_copy(inv, invf.at[yy], r_inv).start()

    def spread(k):
        k = k * 13 % CHIPS
        return (x + k // NZ) % NX * NZ + (z + k) % NZ

    def send_new(k, _):
        d = spread(k)
        j = tile_of(d // NZ, d % NZ)

        @pl.when(j < TILES)
        def _():
            remote(
                comp.at[:, pl.ds(pl.multiple_of(j * 128, 128), 128)],
                nr.at[pl.ds(pl.multiple_of(chip * CAP, CAP), CAP), :],
                s_nr, r_nr, peer(d),
            ).start()

        return 0

    lax.fori_loop(1, CHIPS, send_new, 0)

    @pl.when(holder)
    def _():
        pltpu.make_async_copy(
            comp.at[:, pl.ds(pl.multiple_of(jt * 128, 128), 128)],
            nr.at[pl.ds(pl.multiple_of(chip * CAP, CAP), CAP), :],
            r_nr,
        ).start()

    @pl.when(chip == 0)
    def _():
        def send_orig(xx, zz, dst, sem, to):
            cols = pl.ds(tile_of(xx, zz) * 128, 128)
            remote(mat.at[pl.ds(0, BLOCK), cols], dst, s_or, sem, to).start()

        mine = orig.at[my_half, :]
        send_orig(1, 0, mine, r_or, at(1, 0, core))
        send_orig(2, 0, relay.at[0], r_relay.at[0], at(3, 0, core))
        for zz in AWAY:
            send_orig(1, zz, relay.at[zz], r_relay.at[zz], at(1, 0, core))
            send_orig(3, zz, relay.at[zz], r_relay.at[zz], at(3, 0, core))
            send_orig(2, zz, mine, r_or, at(2, zz, core))
        for zz in AWAY:
            send_orig(0, zz, mine, r_or, at(0, zz, core))

    for k in range(1, NY):
        remote(lp, lg.at[yy], s_y.at[1], r_lp, {"prow": me, "pcol": (yy + k) % NY}).start()
    pltpu.make_async_copy(lp, lg.at[yy], r_lp).start()

    nr[pl.ds(CHIPS * CAP, 8), :] = jnp.zeros((8, 128), f32)


    drain(invf, r_inv)
    i_hi, i_lo = split(invf[...].reshape(NB, NB))
    inv_cat[...] = jnp.concatenate([i_hi, i_lo, i_hi], axis=1)

    @pl.when(holder)
    def _():
        drain(nr.at[pl.ds(0, CHIPS * CAP), :], r_nr)

        def arrange(b, _):
            for t in range(8):
                i = b * 8 + t
                top[pl.ds(i, 1), :] = nr[pl.ds(tab[0, i], 1), :]
            return 0

        lax.fori_loop(0, NB // 8, arrange, 0)
        t_hi, t_lo = split(top[...])
        top[...] = jnp.dot(inv_cat[...], jnp.concatenate([t_hi, t_hi, t_lo], axis=0), preferred_element_type=f32)

        def finish(c):
            own, other = (pl.ds(*SHARE[c]), pl.ds(*SHARE[1 - c]))
            part = psib.at[pl.ds(0, SHARE[c][1])]
            out = remote(top.at[other], psib.at[pl.ds(0, SHARE[1 - c][1])], s_sib.at[0], r_psib, sibling)
            out.start()
            drain(part, r_psib)
            u[jt, own, :] = top[own, :] + part[...]
            out.wait_send()

        pl.when(core == 0)(lambda: finish(0))
        pl.when(core == 1)(lambda: finish(1))

    for c in range(2):

        @pl.when(jnp.logical_not(holder) & (core == c))
        def _():
            u[jt, pl.ds(*SHARE[c]), :] = jnp.zeros((SHARE[c][1], 128), f32)

    def rows_of(c, part=None):
        start, size = SHARE[c]
        return pl.ds(start, size) if part is None else pl.ds(start + part * (size // 2), size // 2)

    def push(c, xx, zz, part, tx, tz):
        j = tile_of(xx, zz)
        ref = u.at[j, rows_of(c, part), :]
        remote(ref, ref, s_ring, r_tile.at[j], at(tx, tz, core)).start()

    def share(c, xx, zz):
        j = tile_of(xx, zz)
        ref = u.at[j, rows_of(c), :]
        remote(ref, ref, s_sib.at[1], r_usib, sibling).start()

    def arrived(c, xx, zz):
        j = tile_of(xx, zz)
        drain(u.at[j, rows_of(c), :], r_tile.at[j])

    xp, xm, xf = (x + 1) % NX, (x + NX - 1) % NX, (x + 2) % NX
    zp, zm = (z + 1) % NZ, (z + NZ - 1) % NZ

    def swap_halves():
        ref = orig.at[my_half, :]
        return remote(ref, ref, s_sib.at[2], r_osib, sibling)

    def swap_first():
        @pl.when(holder)
        def _():
            drain(orig.at[my_half, :], r_or)
            swap_halves().start()

    def give_back():
        @pl.when(holder)
        def _():
            swap_halves().wait()

            def arrange(b, _):
                for t in range(8):
                    i = b * 8 + t
                    ret[pl.ds(i, 1), :] = orig[pl.ds(tab[1, i], 1), :]
                return 0

            lax.fori_loop(0, CHIPS * CAP // 8, arrange, 0)

            def send(k, _):
                d = spread(k)
                remote(ret.at[pl.ds(pl.multiple_of(d * CAP, CAP), CAP), :], sw.at[jt], s_ret, r_ret, peer(d)).start()
                return 0

            lax.fori_loop(1, CHIPS, send, 0)
            pltpu.make_async_copy(ret.at[pl.ds(pl.multiple_of(chip * CAP, CAP), CAP), :], sw.at[jt], r_ret).start()

    def x_neighbours(zz):
        arrived(0, xm, zz)
        push(0, xm, zz, 0, xp, z)
        share(0, xm, zz)
        arrived(0, xp, zz)
        push(0, xp, zz, 1, xm, z)
        share(0, xp, zz)

    def x_far(zz):
        arrived(0, xf, zz)
        share(0, xf, zz)

    def z_step(xx, s):
        for sign in (1, -1):
            zz = (z - sign * s + NZ) % NZ
            if s == NZ // 2 and sign == -1:
                continue
            arrived(1, xx, zz)
            if s < NZ // 2 - 1:
                push(1, xx, zz, None, x, (z + sign + NZ) % NZ)
            elif s == NZ // 2 - 1:
                push(1, xx, zz, 0 if sign == 1 else 1, x, (z + sign + NZ) % NZ)
            share(1, xx, zz)

    def begin(c):
        push(c, x, z, None, x, zp)
        push(c, x, z, None, x, zm)
        push(c, x, z, None, xp, z)
        push(c, x, z, None, xm, z)
        if c == 0:
            push(c, x, z, None, x, (z + 2) % NZ)
            push(c, x, z, None, x, (z + NZ - 2) % NZ)
        else:
            push(c, x, z, None, xf, z)
        share(c, x, z)

    pl.when(core == 0)(lambda: begin(0))
    pl.when(core == 1)(lambda: begin(1))

    def hand_on(zz):
        @pl.when((z == 0) & ((x == 3) | ((x == 1) & (zz > 0))))
        def _():
            drain(relay.at[zz], r_relay.at[zz])
            to = at(x, zz, core) if zz > 0 else at(2, 0, core)
            remote(relay.at[zz], orig.at[my_half, :], s_relay, r_or, to).start()

    hand_on(0)
    for zz in AWAY[:3]:
        hand_on(zz)

    def back(s):
        return (z + NZ - s) % NZ

    def onward(zz):
        push(0, x, zz, None, xp, z)
        push(0, x, zz, None, xm, z)
        share(0, x, zz)

    @pl.when(core == 0)
    def _():
        for s in (2, -2):
            arrived(0, x, back(s))
            push(0, x, back(s), None, x, back(-s // 2))
            push(0, x, back(s), 0 if s > 0 else 1, x, back(-s))
            onward(back(s))
        for s in (1, -1):
            arrived(0, x, back(s))
            onward(back(s))
        for zz in AWAY[3:]:
            hand_on(zz)
        x_neighbours(z)
        for s in (3, -3):
            arrived(0, x, back(s))
            onward(back(s))
        swap_first()
        for s in (2, -2):
            x_neighbours(back(s))
        arrived(0, x, back(4))
        onward(back(4))
        for s in (1, -1):
            x_neighbours(back(s))
        x_far(z)
        give_back()
        for s in (3, -3):
            x_neighbours(back(s))
        for s in (2, -2, 1, -1):
            x_far(back(s))
        x_neighbours(back(4))
        for s in (3, -3, 4):
            x_far(back(s))

    @pl.when(core == 1)
    def _():
        for xx in (xm, xp, xf):
            arrived(1, xx, z)
            push(1, xx, z, None, x, zp)
            push(1, xx, z, None, x, zm)
            share(1, xx, z)
        for zz in AWAY[3:]:
            hand_on(zz)
        for s in range(1, NZ // 2 + 1):
            for xx in (x, xm, xp, xf):
                z_step(xx, s)
            if s == 1:
                swap_first()
            if s == 2:
                give_back()

    drain(lg, r_lp)
    drain(sw.at[pl.ds(0, TILES)], r_ret)
    def end(c):
        drain(u.at[pl.ds(0, CHIPS), pl.ds(*SHARE[1 - c]), :], r_usib)
        drain(u.at[pl.ds(0, CHIPS), pl.ds(*SHARE[c]), :], s_sib.at[1])
        drain(u.at[pl.ds(0, CHIPS - 1), pl.ds(*SHARE[c]), :], s_ring)

    pl.when(core == 0)(lambda: end(0))
    pl.when(core == 1)(lambda: end(1))
    drain(invf.at[pl.ds(0, NY - 1)], s_y.at[0])
    drain(lg.at[pl.ds(0, NY - 1)], s_y.at[1])

    @pl.when(holder)
    def _():
        drain(nr.at[pl.ds(0, (TILES - 1) * CAP), :], s_nr)
        drain(ret.at[pl.ds(0, (CHIPS - 1) * CAP), :], s_ret)

    @pl.when(jnp.logical_not(holder))
    def _():
        drain(nr.at[pl.ds(0, TILES * CAP), :], s_nr)

    @pl.when((z == 0) & (x == 1))
    def _():
        drain(relay.at[pl.ds(1, NZ - 1)], s_relay)

    @pl.when((z == 0) & (x == 3))
    def _():
        drain(relay, s_relay)

    @pl.when(chip == 0)
    def _():
        drain(mat.at[pl.ds(0, BLOCK), :], s_or)


def move(tab, comp, matrix, lower_panel, inverse):
    vm = pl.BlockSpec(memory_space=pltpu.VMEM)
    dma = pltpu.SemaphoreType.DMA
    return pl.pallas_call(
        move_kernel,
        out_shape=(
            jax.ShapeDtypeStruct((CHIPS, NB, 128), f32),
            jax.ShapeDtypeStruct((CHIPS, CAP, 128), f32),
            jax.ShapeDtypeStruct((NY, ROWS // NY, NB), f32),
        ),
        in_specs=[pl.BlockSpec(memory_space=pltpu.SMEM), vm, pl.BlockSpec(memory_space=pl.ANY), vm, vm],
        out_specs=(vm, vm, vm),
        scratch_shapes=[
            pltpu.VMEM((CHIPS * CAP + 8, 128), f32),
            pltpu.VMEM((NB, 128), f32),
            pltpu.VMEM((max(SHARE[0][1], SHARE[1][1]), 128), f32),
            pltpu.VMEM((NY, NB // NY, NB), f32),
            pltpu.VMEM((NB, 128), f32),
            pltpu.VMEM((CHIPS * CAP, 128), f32),
            dma, dma, dma, dma, dma((2,)), dma, dma, dma((3,)), dma, dma, dma, dma, dma, dma((CHIPS,)), dma,
            pltpu.VMEM((NZ, BLOCK, 128), f32), dma, dma((NZ,)),
            pltpu.VMEM((NB, 3 * NB), bf16),
        ],
        compiler_params=pltpu.CompilerParams(collective_id=0, has_side_effects=True, vmem_limit_bytes=16 << 20),
        name="move",
    )(tab, comp, matrix, lower_panel, inverse)


def split(v):
    hi = v.astype(bf16)
    return hi, (v - hi.astype(f32)).astype(bf16)


def update_kernel(tab, mat, u, sw, lg, out, l_cat):
    me = lax.axis_index("prow")

    @pl.when(pl.program_id(0) == 0)
    def _():
        hi, lo = split(lg[...])
        l_cat[...] = jnp.concatenate([hi, lo, hi], axis=1)

    first = pl.program_id(0) * STEP
    cols = pl.ds(pl.multiple_of(first * 128, 128), STEP * 128)
    u_hi, u_lo = split(jnp.concatenate([u[first + k] for k in range(STEP)], axis=1))
    out[...] = mat[:, cols] - jnp.dot(l_cat[...], jnp.concatenate([u_hi, u_hi, u_lo], axis=0), preferred_element_type=f32)
    for k in range(CAP):
        row = tab[3, k]

        @pl.when(row >= 0)
        def _():
            new = jnp.concatenate([sw[first + t, k : k + 1, :] for t in range(STEP)], axis=1)
            out[pl.ds(row, 1), :] = out[pl.ds(row, 1), :] + (new - mat[pl.ds(row, 1), cols])

    for half in range(2):

        @pl.when(me == half)
        def _():
            for k in range(STEP):
                out[0:BLOCK, k * 128 : (k + 1) * 128] = u[first + k, half * BLOCK : (half + 1) * BLOCK, :]


def update(tab, matrix, u, sw, lg):
    vm = pl.BlockSpec(memory_space=pltpu.VMEM)
    return pl.pallas_call(
        update_kernel,
        grid=(TILES // STEP,),
        out_shape=jax.ShapeDtypeStruct((ROWS, COLS), f32),
        in_specs=[pl.BlockSpec(memory_space=pltpu.SMEM), vm, vm, vm, vm],
        out_specs=pl.BlockSpec((ROWS, STEP * 128), lambda g: (0, g)),
        scratch_shapes=[pltpu.VMEM((ROWS, 3 * NB), bf16)],
        compiler_params=pltpu.CompilerParams(vmem_limit_bytes=32 << 20),
        name="update",
    )(tab, matrix, u, sw, lg)


def total(value, axis, size):
    step = 1
    while step < size:
        value = value + lax.ppermute(value, axis, [(i, i ^ step) for i in range(size)])
        step *= 2
    return value


def general(matrix, lg, inverse, source, moved):
    my_row = lax.axis_index("prow")
    row_count = lax.axis_size("prow")
    high = functools.partial(jnp.dot, precision=lax.Precision.HIGHEST, preferred_element_type=f32)
    local_rows = jnp.arange(ROWS, dtype=i32)
    global_rows = (local_rows // BLOCK * row_count + my_row) * BLOCK + local_rows % BLOCK
    owner = source // BLOCK % row_count
    local_index = source // BLOCK // row_count * BLOCK + source % BLOCK
    new_part = jnp.where((owner == my_row)[:, None], jnp.take(matrix, local_index, axis=0), 0.0)
    block_ids = jnp.arange(NB // BLOCK, dtype=i32)
    orig_part = jnp.where((block_ids == my_row)[:, None, None], matrix[None, :BLOCK], 0.0).reshape(NB, COLS)
    gathered, top_orig = jnp.split(total(jnp.concatenate([new_part, orig_part]), "prow", N_PROW), 2)
    hit = (source[None, :] == global_rows[:, None]) & (global_rows >= NB)[:, None]
    fetch = jnp.max(jnp.where(hit, moved[None, :], -1), axis=1)
    swapped = jnp.where((fetch >= 0)[:, None], jnp.take(top_orig, jnp.clip(fetch, 0, NB - 1), axis=0), matrix)
    parts = jnp.where((jnp.arange(NY) == lax.axis_index("pcol"))[:, None, None], inverse[None], 0.0)
    u_rows = high(total(parts.reshape(NB, NB), "pcol", NY), gathered)
    result = swapped - high(lg, u_rows)
    head = lax.dynamic_slice_in_dim(u_rows, jnp.minimum(my_row, 1) * BLOCK, BLOCK, 0)
    first = jnp.where(my_row < 2, head, result[:BLOCK])
    return jnp.concatenate([first, result[BLOCK:]], axis=0)


def local(matrix, lower_panel, inverse, pivots):
    tab, comp, crowded = plan(pivots, matrix)
    u, sw, lg = move(tab, comp, matrix, lower_panel, inverse)
    lg = lg.reshape(ROWS, NB)
    result = update(tab, matrix, u, sw, lg)
    _, result = lax.while_loop(
        lambda state: state[0] > 0,
        lambda state: (jnp.int32(0), general(matrix, lg, inverse, tab[4, :NB], tab[5, :NB])),
        (crowded[0, 0], result),
    )
    return result


def solution(mesh):
    return jax.shard_map(
        local,
        mesh=mesh,
        in_specs=(P("prow", "pcol"), P(("prow", "pcol"), None), P("pcol", None), P()),
        out_specs=P("prow", "pcol"),
        check_vma=False,
    )
```

```python
import functools

import jax
import jax.numpy as jnp
from jax import lax
from jax.experimental import pallas as pl
from jax.experimental.pallas import tpu as pltpu
from jax.sharding import PartitionSpec as P

BLOCK = 128
NB = 256
CAP = 16
NX, NZ, NY = 4, 8, 4
N_PROW = 64
CHIPS = NX * NZ
STEP = 15
SHARE = ((0, 112), (112, 144))
AWAY = (4, 3, 5, 2, 6, 1, 7)
TILES = 30
COLS = TILES * 128
ROWS = 384
MESH = pl.DeviceIdType.MESH
f32 = jnp.float32
i32 = jnp.int32
bf16 = jnp.bfloat16


def plan_kernel(p_ref, mat, tab, comp, crowded, tab_s, sem, row_sems):
    me = lax.axis_index("prow")
    core = (me % 2).astype(f32)
    mef = me.astype(f32)
    big = (NB, NB)
    I = lax.broadcasted_iota(i32, big, 0)
    J = lax.broadcasted_iota(i32, big, 1)
    Jf = J.astype(f32)
    eye = I == J
    lt = J < I
    PB = jnp.broadcast_to(p_ref[...].astype(f32), big)

    def to_col(row_b):
        return jnp.sum(jnp.where(eye, row_b, 0.0), axis=1, keepdims=True)

    def to_row(col):
        return jnp.sum(jnp.where(eye, jnp.broadcast_to(col, big), 0.0), axis=0, keepdims=True)

    def pick(col_idx, row_vals):
        return jnp.sum(jnp.where(Jf == col_idx, jnp.broadcast_to(row_vals, big), 0.0), axis=1, keepdims=True)

    p_col = to_col(PB)
    eq = (p_col == PB) & lt
    prev = jnp.max(jnp.where(eq, Jf, -1.0), axis=1, keepdims=True)
    later = jnp.max(jnp.where(eq, 1.0, 0.0), axis=0, keepdims=True)
    par = jnp.max(jnp.where((PB == I.astype(f32)) & lt, Jf, -1.0), axis=1, keepdims=True)
    icol = lax.broadcasted_iota(i32, (NB, 1), 0).astype(f32)
    root = jnp.where(par < 0.0, icol, par)

    def more(state):
        return state[1] > 0.0

    def double(state):
        r, _ = state
        nr = pick(r, to_row(r))
        return nr, jnp.max(r - nr)

    root, _ = lax.while_loop(more, double, (root, jnp.float32(1.0)))
    c_row = to_row(root)
    ts = jnp.where(prev >= 0.0, pick(prev, c_row), p_col)
    tsi = ts.astype(i32)
    owner_i = lax.shift_right_logical(tsi, 7) & 63
    owner = owner_i.astype(f32)
    lidx = (lax.shift_right_logical(tsi, 13) * BLOCK + (tsi & 127)).astype(f32)
    slot = jnp.sum(jnp.where((owner == jnp.broadcast_to(to_row(owner), big)) & lt, 1.0, 0.0), axis=1, keepdims=True)
    last_c = jnp.broadcast_to(jnp.where(later > 0.0, 0.0, c_row), big)
    w = jnp.sum(jnp.where(ts == PB, last_c, 0.0), axis=1, keepdims=True)
    out_row = ts >= float(NB)
    flag = jnp.max(slot) >= float(CAP)
    mine_core = (owner_i & 1).astype(f32) == core
    chip = lax.shift_right_logical(owner_i, 1).astype(f32)
    flat = jnp.where(mine_core, chip * CAP + slot, float(CHIPS * CAP))
    flat = jnp.minimum(flat, float(CHIPS * CAP))
    src_row = to_row(flat)
    S = lax.broadcasted_iota(i32, (NB, CHIPS * CAP), 1).astype(f32)
    ret = jnp.sum(jnp.where((flat == S) & (slot < float(CAP)) & out_row, w, 0.0), axis=0, keepdims=True)
    ret = jnp.clip(ret, 0.0, NB - 1.0)
    K = lax.broadcasted_iota(i32, (NB, 128), 1).astype(f32)
    own = (owner == mef) & (slot == K)
    gath = jnp.max(jnp.where(own, lidx, 0.0), axis=0, keepdims=True)
    dest = jnp.max(jnp.where(own & out_row, lidx, -1.0), axis=0, keepdims=True)
    tab[...] = jnp.zeros((8, 512), i32)
    tab[0:1, 0:NB] = src_row.astype(i32)
    tab[1:2, :] = ret.astype(i32)
    tab[2:3, 0:128] = gath.astype(i32)
    tab[3:4, 0:128] = dest.astype(i32)
    tab[4:5, 0:NB] = to_row(ts).astype(i32)
    tab[5:6, 0:NB] = to_row(w).astype(i32)
    crowded[0, 0] = jnp.where(flag, 1, 0)
    copy = pltpu.make_async_copy(tab.at[2:3, 0:128], tab_s, sem)
    copy.start()
    copy.wait()
    copies = []
    for k in range(CAP):
        row = tab_s[0, k]
        copies.append(pltpu.make_async_copy(mat.at[pl.ds(row, 1), :], comp.at[pl.ds(k, 1), :], row_sems.at[k]))
    for copy in copies:
        copy.start()
    for copy in copies:
        copy.wait()


def plan(pivots, matrix):
    vm = pl.BlockSpec(memory_space=pltpu.VMEM)
    return pl.pallas_call(
        plan_kernel,
        out_shape=(
            jax.ShapeDtypeStruct((8, 512), i32),
            jax.ShapeDtypeStruct((CAP, COLS), f32),
            jax.ShapeDtypeStruct((1, 1), i32),
        ),
        in_specs=[vm, pl.BlockSpec(memory_space=pl.ANY)],
        out_specs=(vm, vm, pl.BlockSpec(memory_space=pltpu.SMEM)),
        scratch_shapes=[
            pltpu.SMEM((1, 128), i32),
            pltpu.SemaphoreType.DMA,
            pltpu.SemaphoreType.DMA((CAP,)),
        ],
        compiler_params=pltpu.CompilerParams(vmem_limit_bytes=16 << 20),
        name="plan",
    )(pivots.reshape(1, NB), matrix)


def move_kernel(tab, comp, mat, lp, inv, u, sw, lg, nr, top, psib, invf, orig, ret,
                s_nr, r_nr, s_or, r_or, s_y, r_inv, r_lp, s_sib, r_psib, r_osib, s_ret, r_ret, s_ring, r_tile, r_usib,
                relay, s_relay, r_relay, inv_cat):
    me = lax.axis_index("prow")
    yy = lax.axis_index("pcol")
    core = me % 2
    chip = me // 2
    x = chip // NZ
    z = chip % NZ

    def tile_of(xx, zz):
        return (zz + NZ - 1) % NZ * NX + (xx + NX - 1) % NX

    def at(xx, zz, cc):
        return {"prow": (xx * NZ + zz) * 2 + cc, "pcol": yy}

    def peer(dchip):
        return {"prow": dchip * 2 + core, "pcol": yy}

    my_half = pl.ds(pl.multiple_of(core * BLOCK, BLOCK), BLOCK)
    sibling = at(x, z, 1 - core)
    jt = tile_of(x, z)
    holder = jt < TILES

    def remote(src, dst, ss, rs, dev):
        return pltpu.make_async_remote_copy(src_ref=src, dst_ref=dst, send_sem=ss, recv_sem=rs, device_id=dev, device_id_type=MESH)

    def drain(ref, sem):
        pltpu.make_async_copy(ref, ref, sem).wait()

    barrier = pltpu.get_barrier_semaphore()

    def greet(k, _):
        pl.semaphore_signal(barrier, inc=1, device_id=peer((chip + k) % CHIPS), device_id_type=MESH)
        return 0

    lax.fori_loop(1, CHIPS, greet, 0)
    pl.semaphore_signal(barrier, inc=1, device_id=sibling, device_id_type=MESH)
    for k in range(1, NY):
        pl.semaphore_signal(barrier, inc=1, device_id={"prow": me, "pcol": (yy + k) % NY}, device_id_type=MESH)
    pl.semaphore_wait(barrier, CHIPS - 1 + 1 + NY - 1)

    for k in range(1, NY):
        remote(inv, invf.at[yy], s_y.at[0], r_inv, {"prow": me, "pcol": (yy + k) % NY}).start()
    pltpu.make_async_copy(inv, invf.at[yy], r_inv).start()

    def spread(k):
        k = k * 13 % CHIPS
        return (x + k // NZ) % NX * NZ + (z + k) % NZ

    def send_new(k, _):
        d = spread(k)
        j = tile_of(d // NZ, d % NZ)

        @pl.when(j < TILES)
        def _():
            remote(
                comp.at[:, pl.ds(pl.multiple_of(j * 128, 128), 128)],
                nr.at[pl.ds(pl.multiple_of(chip * CAP, CAP), CAP), :],
                s_nr, r_nr, peer(d),
            ).start()

        return 0

    lax.fori_loop(1, CHIPS, send_new, 0)

    @pl.when(holder)
    def _():
        pltpu.make_async_copy(
            comp.at[:, pl.ds(pl.multiple_of(jt * 128, 128), 128)],
            nr.at[pl.ds(pl.multiple_of(chip * CAP, CAP), CAP), :],
            r_nr,
        ).start()

    @pl.when(chip == 0)
    def _():
        def send_orig(xx, zz, dst, sem, to):
            cols = pl.ds(tile_of(xx, zz) * 128, 128)
            remote(mat.at[pl.ds(0, BLOCK), cols], dst, s_or, sem, to).start()

        mine = orig.at[my_half, :]
        send_orig(1, 0, mine, r_or, at(1, 0, core))
        send_orig(2, 0, relay.at[0], r_relay.at[0], at(3, 0, core))
        for zz in AWAY:
            send_orig(1, zz, relay.at[zz], r_relay.at[zz], at(1, 0, core))
            send_orig(3, zz, relay.at[zz], r_relay.at[zz], at(3, 0, core))
            send_orig(2, zz, mine, r_or, at(2, zz, core))
        for zz in AWAY:
            send_orig(0, zz, mine, r_or, at(0, zz, core))

    for k in range(1, NY):
        remote(lp, lg.at[yy], s_y.at[1], r_lp, {"prow": me, "pcol": (yy + k) % NY}).start()
    pltpu.make_async_copy(lp, lg.at[yy], r_lp).start()

    nr[pl.ds(CHIPS * CAP, 8), :] = jnp.zeros((8, 128), f32)


    drain(invf, r_inv)
    i_hi, i_lo = split(invf[...].reshape(NB, NB))
    inv_cat[...] = jnp.concatenate([i_hi, i_lo, i_hi], axis=1)

    @pl.when(holder)
    def _():
        drain(nr.at[pl.ds(0, CHIPS * CAP), :], r_nr)

        def arrange(b, _):
            for t in range(8):
                i = b * 8 + t
                top[pl.ds(i, 1), :] = nr[pl.ds(tab[0, i], 1), :]
            return 0

        lax.fori_loop(0, NB // 8, arrange, 0)
        t_hi, t_lo = split(top[...])
        top[...] = jnp.dot(inv_cat[...], jnp.concatenate([t_hi, t_hi, t_lo], axis=0), preferred_element_type=f32)

        def finish(c):
            own, other = (pl.ds(*SHARE[c]), pl.ds(*SHARE[1 - c]))
            part = psib.at[pl.ds(0, SHARE[c][1])]
            out = remote(top.at[other], psib.at[pl.ds(0, SHARE[1 - c][1])], s_sib.at[0], r_psib, sibling)
            out.start()
            drain(part, r_psib)
            u[jt, own, :] = top[own, :] + part[...]
            out.wait_send()

        pl.when(core == 0)(lambda: finish(0))
        pl.when(core == 1)(lambda: finish(1))

    for c in range(2):

        @pl.when(jnp.logical_not(holder) & (core == c))
        def _():
            u[jt, pl.ds(*SHARE[c]), :] = jnp.zeros((SHARE[c][1], 128), f32)

    def rows_of(c, part=None):
        start, size = SHARE[c]
        return pl.ds(start, size) if part is None else pl.ds(start + part * (size // 2), size // 2)

    def push(c, xx, zz, part, tx, tz):
        j = tile_of(xx, zz)
        ref = u.at[j, rows_of(c, part), :]
        remote(ref, ref, s_ring, r_tile.at[j], at(tx, tz, core)).start()

    def share(c, xx, zz):
        j = tile_of(xx, zz)
        ref = u.at[j, rows_of(c), :]
        remote(ref, ref, s_sib.at[1], r_usib, sibling).start()

    def arrived(c, xx, zz):
        j = tile_of(xx, zz)
        drain(u.at[j, rows_of(c), :], r_tile.at[j])

    xp, xm, xf = (x + 1) % NX, (x + NX - 1) % NX, (x + 2) % NX
    zp, zm = (z + 1) % NZ, (z + NZ - 1) % NZ

    def swap_halves():
        ref = orig.at[my_half, :]
        return remote(ref, ref, s_sib.at[2], r_osib, sibling)

    def swap_first():
        @pl.when(holder)
        def _():
            drain(orig.at[my_half, :], r_or)
            swap_halves().start()

    def give_back():
        @pl.when(holder)
        def _():
            swap_halves().wait()

            def arrange(b, _):
                for t in range(8):
                    i = b * 8 + t
                    ret[pl.ds(i, 1), :] = orig[pl.ds(tab[1, i], 1), :]
                return 0

            lax.fori_loop(0, CHIPS * CAP // 8, arrange, 0)

            def send(k, _):
                d = spread(k)
                remote(ret.at[pl.ds(pl.multiple_of(d * CAP, CAP), CAP), :], sw.at[jt], s_ret, r_ret, peer(d)).start()
                return 0

            lax.fori_loop(1, CHIPS, send, 0)
            pltpu.make_async_copy(ret.at[pl.ds(pl.multiple_of(chip * CAP, CAP), CAP), :], sw.at[jt], r_ret).start()

    def x_neighbours(zz):
        arrived(0, xm, zz)
        push(0, xm, zz, 0, xp, z)
        share(0, xm, zz)
        arrived(0, xp, zz)
        push(0, xp, zz, 1, xm, z)
        share(0, xp, zz)

    def x_far(zz):
        arrived(0, xf, zz)
        share(0, xf, zz)

    def z_step(xx, s):
        for sign in (1, -1):
            zz = (z - sign * s + NZ) % NZ
            if s == NZ // 2 and sign == -1:
                continue
            arrived(1, xx, zz)
            if s < NZ // 2 - 1:
                push(1, xx, zz, None, x, (z + sign + NZ) % NZ)
            elif s == NZ // 2 - 1:
                push(1, xx, zz, 0 if sign == 1 else 1, x, (z + sign + NZ) % NZ)
            share(1, xx, zz)

    def begin(c):
        push(c, x, z, None, x, zp)
        push(c, x, z, None, x, zm)
        push(c, x, z, None, xp, z)
        push(c, x, z, None, xm, z)
        if c == 0:
            push(c, x, z, None, x, (z + 2) % NZ)
            push(c, x, z, None, x, (z + NZ - 2) % NZ)
        else:
            push(c, x, z, None, xf, z)
        share(c, x, z)

    pl.when(core == 0)(lambda: begin(0))
    pl.when(core == 1)(lambda: begin(1))

    def hand_on(zz):
        @pl.when((z == 0) & ((x == 3) | ((x == 1) & (zz > 0))))
        def _():
            drain(relay.at[zz], r_relay.at[zz])
            to = at(x, zz, core) if zz > 0 else at(2, 0, core)
            remote(relay.at[zz], orig.at[my_half, :], s_relay, r_or, to).start()

    hand_on(0)
    for zz in AWAY[:3]:
        hand_on(zz)

    def back(s):
        return (z + NZ - s) % NZ

    def onward(zz):
        push(0, x, zz, None, xp, z)
        push(0, x, zz, None, xm, z)
        share(0, x, zz)

    @pl.when(core == 0)
    def _():
        for s in (2, -2):
            arrived(0, x, back(s))
            push(0, x, back(s), None, x, back(-s // 2))
            push(0, x, back(s), 0 if s > 0 else 1, x, back(-s))
            onward(back(s))
        for s in (1, -1):
            arrived(0, x, back(s))
            onward(back(s))
        for zz in AWAY[3:]:
            hand_on(zz)
        x_neighbours(z)
        for s in (3, -3):
            arrived(0, x, back(s))
            onward(back(s))
        swap_first()
        for s in (2, -2):
            x_neighbours(back(s))
        arrived(0, x, back(4))
        onward(back(4))
        for s in (1, -1):
            x_neighbours(back(s))
        x_far(z)
        give_back()
        for s in (3, -3):
            x_neighbours(back(s))
        for s in (2, -2, 1, -1):
            x_far(back(s))
        x_neighbours(back(4))
        for s in (3, -3, 4):
            x_far(back(s))

    @pl.when(core == 1)
    def _():
        for xx in (xm, xp, xf):
            arrived(1, xx, z)
            push(1, xx, z, None, x, zp)
            push(1, xx, z, None, x, zm)
            share(1, xx, z)
        for zz in AWAY[3:]:
            hand_on(zz)
        for s in range(1, NZ // 2 + 1):
            for xx in (x, xm, xp, xf):
                z_step(xx, s)
            if s == 1:
                swap_first()
            if s == 2:
                give_back()

    drain(lg, r_lp)
    drain(sw.at[pl.ds(0, TILES)], r_ret)
    def end(c):
        drain(u.at[pl.ds(0, CHIPS), pl.ds(*SHARE[1 - c]), :], r_usib)
        drain(u.at[pl.ds(0, CHIPS), pl.ds(*SHARE[c]), :], s_sib.at[1])
        drain(u.at[pl.ds(0, CHIPS - 1), pl.ds(*SHARE[c]), :], s_ring)

    pl.when(core == 0)(lambda: end(0))
    pl.when(core == 1)(lambda: end(1))
    drain(invf.at[pl.ds(0, NY - 1)], s_y.at[0])
    drain(lg.at[pl.ds(0, NY - 1)], s_y.at[1])

    @pl.when(holder)
    def _():
        drain(nr.at[pl.ds(0, (TILES - 1) * CAP), :], s_nr)
        drain(ret.at[pl.ds(0, (CHIPS - 1) * CAP), :], s_ret)

    @pl.when(jnp.logical_not(holder))
    def _():
        drain(nr.at[pl.ds(0, TILES * CAP), :], s_nr)

    @pl.when((z == 0) & (x == 1))
    def _():
        drain(relay.at[pl.ds(1, NZ - 1)], s_relay)

    @pl.when((z == 0) & (x == 3))
    def _():
        drain(relay, s_relay)

    @pl.when(chip == 0)
    def _():
        drain(mat.at[pl.ds(0, BLOCK), :], s_or)


def move(tab, comp, matrix, lower_panel, inverse):
    vm = pl.BlockSpec(memory_space=pltpu.VMEM)
    dma = pltpu.SemaphoreType.DMA
    return pl.pallas_call(
        move_kernel,
        out_shape=(
            jax.ShapeDtypeStruct((CHIPS, NB, 128), f32),
            jax.ShapeDtypeStruct((CHIPS, CAP, 128), f32),
            jax.ShapeDtypeStruct((NY, ROWS // NY, NB), f32),
        ),
        in_specs=[pl.BlockSpec(memory_space=pltpu.SMEM), vm, pl.BlockSpec(memory_space=pl.ANY), vm, vm],
        out_specs=(vm, vm, vm),
        scratch_shapes=[
            pltpu.VMEM((CHIPS * CAP + 8, 128), f32),
            pltpu.VMEM((NB, 128), f32),
            pltpu.VMEM((max(SHARE[0][1], SHARE[1][1]), 128), f32),
            pltpu.VMEM((NY, NB // NY, NB), f32),
            pltpu.VMEM((NB, 128), f32),
            pltpu.VMEM((CHIPS * CAP, 128), f32),
            dma, dma, dma, dma, dma((2,)), dma, dma, dma((3,)), dma, dma, dma, dma, dma, dma((CHIPS,)), dma,
            pltpu.VMEM((NZ, BLOCK, 128), f32), dma, dma((NZ,)),
            pltpu.VMEM((NB, 3 * NB), bf16),
        ],
        compiler_params=pltpu.CompilerParams(collective_id=0, has_side_effects=True, vmem_limit_bytes=16 << 20),
        name="move",
    )(tab, comp, matrix, lower_panel, inverse)


def split(v):
    hi = v.astype(bf16)
    return hi, (v - hi.astype(f32)).astype(bf16)


def update_kernel(tab, mat, u, sw, lg, out, l_cat):
    me = lax.axis_index("prow")

    @pl.when(pl.program_id(0) == 0)
    def _():
        hi, lo = split(lg[...])
        l_cat[...] = jnp.concatenate([hi, lo, hi], axis=1)

    first = pl.program_id(0) * STEP
    cols = pl.ds(pl.multiple_of(first * 128, 128), STEP * 128)
    u_hi, u_lo = split(jnp.concatenate([u[first + k] for k in range(STEP)], axis=1))
    out[...] = mat[:, cols] - jnp.dot(l_cat[...], jnp.concatenate([u_hi, u_hi, u_lo], axis=0), preferred_element_type=f32)
    for k in range(CAP):
        row = tab[3, k]

        @pl.when(row >= 0)
        def _():
            new = jnp.concatenate([sw[first + t, k : k + 1, :] for t in range(STEP)], axis=1)
            out[pl.ds(row, 1), :] = out[pl.ds(row, 1), :] + (new - mat[pl.ds(row, 1), cols])

    for half in range(2):

        @pl.when(me == half)
        def _():
            for k in range(STEP):
                out[0:BLOCK, k * 128 : (k + 1) * 128] = u[first + k, half * BLOCK : (half + 1) * BLOCK, :]


def update(tab, matrix, u, sw, lg):
    vm = pl.BlockSpec(memory_space=pltpu.VMEM)
    return pl.pallas_call(
        update_kernel,
        grid=(TILES // STEP,),
        out_shape=jax.ShapeDtypeStruct((ROWS, COLS), f32),
        in_specs=[pl.BlockSpec(memory_space=pltpu.SMEM), vm, vm, vm, vm],
        out_specs=pl.BlockSpec((ROWS, STEP * 128), lambda g: (0, g)),
        scratch_shapes=[pltpu.VMEM((ROWS, 3 * NB), bf16)],
        compiler_params=pltpu.CompilerParams(vmem_limit_bytes=32 << 20),
        name="update",
    )(tab, matrix, u, sw, lg)


def total(value, axis, size):
    step = 1
    while step < size:
        value = value + lax.ppermute(value, axis, [(i, i ^ step) for i in range(size)])
        step *= 2
    return value


def general(matrix, lg, inverse, source, moved):
    my_row = lax.axis_index("prow")
    row_count = lax.axis_size("prow")
    high = functools.partial(jnp.dot, precision=lax.Precision.HIGHEST, preferred_element_type=f32)
    local_rows = jnp.arange(ROWS, dtype=i32)
    global_rows = (local_rows // BLOCK * row_count + my_row) * BLOCK + local_rows % BLOCK
    owner = source // BLOCK % row_count
    local_index = source // BLOCK // row_count * BLOCK + source % BLOCK
    new_part = jnp.where((owner == my_row)[:, None], jnp.take(matrix, local_index, axis=0), 0.0)
    block_ids = jnp.arange(NB // BLOCK, dtype=i32)
    orig_part = jnp.where((block_ids == my_row)[:, None, None], matrix[None, :BLOCK], 0.0).reshape(NB, COLS)
    gathered, top_orig = jnp.split(total(jnp.concatenate([new_part, orig_part]), "prow", N_PROW), 2)
    hit = (source[None, :] == global_rows[:, None]) & (global_rows >= NB)[:, None]
    fetch = jnp.max(jnp.where(hit, moved[None, :], -1), axis=1)
    swapped = jnp.where((fetch >= 0)[:, None], jnp.take(top_orig, jnp.clip(fetch, 0, NB - 1), axis=0), matrix)
    parts = jnp.where((jnp.arange(NY) == lax.axis_index("pcol"))[:, None, None], inverse[None], 0.0)
    u_rows = high(total(parts.reshape(NB, NB), "pcol", NY), gathered)
    result = swapped - high(lg, u_rows)
    head = lax.dynamic_slice_in_dim(u_rows, jnp.minimum(my_row, 1) * BLOCK, BLOCK, 0)
    first = jnp.where(my_row < 2, head, result[:BLOCK])
    return jnp.concatenate([first, result[BLOCK:]], axis=0)


def local(matrix, lower_panel, inverse, pivots):
    tab, comp, crowded = plan(pivots, matrix)
    u, sw, lg = move(tab, comp, matrix, lower_panel, inverse)
    lg = lg.reshape(ROWS, NB)
    result = update(tab, matrix, u, sw, lg)
    _, result = lax.while_loop(
        lambda state: state[0] > 0,
        lambda state: (jnp.int32(0), general(matrix, lg, inverse, tab[4, :NB], tab[5, :NB])),
        (crowded[0, 0], result),
    )
    return result


def solution(mesh):
    return jax.shard_map(
        local,
        mesh=mesh,
        in_specs=(P("prow", "pcol"), P(("prow", "pcol"), None), P("pcol", None), P()),
        out_specs=P("prow", "pcol"),
        check_vma=False,
    )
```
